128 devices in a mesh: dp: 16 (over z, x_hi, core), ctx: 8 (over x_lo, y).
Axes of the slice: x: 4 (x_hi: 2, x_lo: 2; x = x_hi * 2 + x_lo), y: 4, z: 4, core: 2. Of those that a mesh axis runs over, the one named last changes fastest.
Arguments:
- queries: bfloat16 [16, 1024, 2048], P('dp', 'ctx'), may hold values from -5 to 5
- keys: bfloat16 [16, 1024, 2048], P('dp', 'ctx'), may hold values from -5 to 5
- values: bfloat16 [16, 1024, 2048], P('dp', 'ctx'), may hold values from -12 to 12
- out_weight: bfloat16 [2048, 2048], P(('dp', 'ctx')), may hold values from -0.5 to 0.5
- cotangent: bfloat16 [16, 1024, 2048], P('dp', 'ctx'), may hold values from -6 to 6
- rand_blocks: int32 [16, 16, 16, 3], P('dp', 'ctx'), may hold values from 0 to 15
- glob_blocks: int32 [16, 2], P('dp'), may hold values from 0 to 15
Outputs:
- mixed: bfloat16 [16, 1024, 2048], P('dp', 'ctx')
- grad_queries: bfloat16 [16, 1024, 2048], P('dp', 'ctx')
- grad_keys: bfloat16 [16, 1024, 2048], P('dp', 'ctx')
- grad_values: bfloat16 [16, 1024, 2048], P('dp', 'ctx')
- grad_weight: float32 [2048, 2048], P(('dp', 'ctx'))
The draws below stay inside these ranges and needn't reach their ends.
Inputs may be any that keep to these rules, and one draw needn't show every extreme that they name: `glob_blocks`: each entry names a block of the document.
All inputs are finite; a program needn't handle non-finite values.
Results may differ from the reference program's by a relative error of at most 0.015.
Values may be sent and summed in bfloat16 or wider, within the bound.
No kernel may reach another device: no remote copies, remote signals or barrier semaphores. Data moves between devices by JAX's collectives and lax.ppermute only.
A program may use at most 128 MiB of HBM per device.

```python
import math
import jax
import jax.numpy as jnp
from jax import lax

H = 16
HS = 128
D_OUT = 2048
BLK = 64
WIN = 1
GLOB = 2
RAND = 3
DOCS = 16
LEN = 1024
NB = 16
HD = 2048


def draw_queries(key, part):
    key = jax.random.fold_in(key, 1)
    base = jax.random.normal(key, (DOCS, LEN, HD), jnp.float32)
    return jnp.clip(base, -5.0, 5.0).astype(jnp.bfloat16)


def draw_keys(key, part):
    key = jax.random.fold_in(key, 2)
    base = jax.random.normal(key, (DOCS, LEN, HD), jnp.float32)
    return jnp.clip(base, -5.0, 5.0).astype(jnp.bfloat16)


def set_ends(values, rng, least, top_value):
    shape = values.shape
    index_at = [jax.random.randint(jax.random.fold_in(rng, axis), (), 0, shape[axis]) for axis in range(len(shape))]
    values = values.at[tuple(index_at)].set(least)
    longest = shape.index(max(shape))
    index_at[longest] = (index_at[longest] + 1) % shape[longest]
    return values.at[tuple(index_at)].set(top_value)


def with_spikes(result, key, source, target, blocks, factor):
    def block_of(axis_at):
        return (jnp.arange(result.shape[axis_at]) // (result.shape[axis_at] // blocks)).reshape((-1,) + (1,) * (result.ndim - 1 - axis_at))

    first = jax.random.permutation(key, blocks)[block_of(target)]
    second = (block_of(target) + blocks // 2) % blocks
    return jnp.where((block_of(source) == first) | (block_of(source) == second), factor * result, result)


def steps_of(rng, extent, shards, least, top_value):
    factor_of = 1.0
    for dim, shards_of in shards:
        steps = jax.random.uniform(jax.random.fold_in(jax.random.fold_in(rng, 6), dim), (shards_of,), jnp.float32, least / len(shards), top_value / len(shards))
        factor_of = factor_of * jnp.repeat(jnp.exp(steps), extent[dim] // shards_of).reshape((-1,) + (1,) * (len(extent) - 1 - dim))
    return factor_of


def normal_values(stream_key, dims, scale, most, cuts=(), held_as=jnp.bfloat16):
    factor_of = steps_of(stream_key, dims, cuts, -0.22, 0.18) if cuts else 1.0
    result = jax.random.normal(stream_key, dims, jnp.float32) * scale * factor_of
    return jnp.minimum(jnp.maximum(result, -most), most).astype(held_as)


def noise_with(own_key, dims, deviation, limit, pieces, heavy, held_as=jnp.bfloat16):
    values = deviation * jax.random.normal(own_key, dims, jnp.float32)
    if pieces:
        values = values * steps_of(own_key, dims, pieces, -0.22, 0.18)
    return jnp.clip(with_spikes(values, jax.random.fold_in(own_key, 3), *heavy), -limit, limit).astype(held_as)


def setup_inputs(seed: int = 0) -> dict:
    key_list = jax.random.split(jax.random.key(seed), 8)
    return {
        "queries": draw_queries(jax.random.fold_in(key_list[7], 71), 0),
        "keys": draw_keys(jax.random.fold_in(key_list[7], 71), 0),
        "values": normal_values(key_list[2], (DOCS, LEN, HD), 2.0, 12.0, ((0, 16), (1, 8))),
        "out_weight": normal_values(key_list[3], (D_OUT, HD), HS ** -0.5, 0.5, ((0, 128),)),
        "cotangent": noise_with(key_list[4], (DOCS, LEN, D_OUT), 1.0, 6.0, ((0, 16), (1, 8)), (0, 2, 16, 2.0)),
        "rand_blocks": set_ends(jax.random.randint(key_list[5], (DOCS, H, NB, RAND), 0, NB), jax.random.fold_in(key_list[5], 1), 0, NB - 1).astype(jnp.int32),
        "glob_blocks": set_ends(jax.random.randint(key_list[6], (DOCS, GLOB), 0, NB), jax.random.fold_in(key_list[6], 1), 0, NB - 1).astype(jnp.int32),
    }


masked_score = -1e+30

def block_lists(rand_rows, glob_row, block_count):
    head_count = rand_rows.shape[0]
    width = 2 * WIN + 1
    offsets = jnp.arange(-WIN, WIN + 1, dtype=jnp.int32)
    window = jnp.arange(block_count, dtype=jnp.int32)[:, None] + offsets[None, :]
    inside = (window >= 0) & (window < block_count)
    window = jnp.clip(window, 0, block_count - 1)
    lists = jnp.concatenate([jnp.broadcast_to(window, (head_count, block_count, width)), jnp.broadcast_to(glob_row.astype(jnp.int32)[None, None, :], (head_count, block_count, glob_row.shape[0])), rand_rows.astype(jnp.int32)], axis=-1)
    in_range = jnp.concatenate([jnp.broadcast_to(inside, (head_count, block_count, width)), jnp.ones((head_count, block_count, lists.shape[-1] - width), dtype=jnp.bool_)], axis=-1)
    positions = jnp.arange(lists.shape[-1], dtype=jnp.int32)
    earlier = positions[None, :] < positions[:, None]
    matching = lists[..., :, None] == lists[..., None, :]
    repeated = jnp.any(matching & earlier & in_range[..., None, :], axis=-1)
    return (lists, in_range & jnp.logical_not(repeated))

def head_pass(query_blocks, key_blocks, value_blocks, cot_blocks, lists, live_entries):
    scale = 1.0 / math.sqrt(HS)
    key_sets = key_blocks[lists].astype(jnp.float32)
    value_sets = value_blocks[lists].astype(jnp.float32)
    query_wide = query_blocks.astype(jnp.float32)
    cot_wide = cot_blocks.astype(jnp.float32)
    live_mask = live_entries[:, None, :, None]
    scores = jnp.einsum('nqd,nekd->nqek', query_wide, key_sets) * scale
    scores = jnp.where(live_mask, scores, masked_score)
    row_max = lax.optimization_barrier(jnp.max(scores, axis=(2, 3), keepdims=True))
    unnormed = jnp.where(live_mask, jnp.exp(scores - row_max), 0.0)
    probs = unnormed / lax.optimization_barrier(jnp.sum(unnormed, axis=(2, 3), keepdims=True))
    probs_low = probs.astype(jnp.bfloat16)
    probs_wide = probs_low.astype(jnp.float32)
    attended = jnp.einsum('nqek,nekd->nqd', probs_wide, value_sets).astype(jnp.bfloat16)
    delta = lax.optimization_barrier(jnp.sum(cot_wide * attended.astype(jnp.float32), axis=-1))
    prob_grad = jnp.einsum('nqd,nekd->nqek', cot_wide, value_sets)
    score_grad = (probs * (prob_grad - delta[:, :, None, None])).astype(jnp.bfloat16).astype(jnp.float32)
    query_grad = (jnp.einsum('nqek,nekd->nqd', score_grad, key_sets) * scale).astype(jnp.bfloat16)
    key_terms = jnp.einsum('nqek,nqd->nekd', score_grad, query_wide) * scale
    value_terms = jnp.einsum('nqek,nqd->nekd', probs_wide, cot_wide)
    flat_lists = lists.reshape(-1)
    block_count = key_blocks.shape[0]
    key_grad = jax.ops.segment_sum(key_terms.reshape(flat_lists.shape[0], -1), flat_lists, num_segments=block_count)
    value_grad = jax.ops.segment_sum(value_terms.reshape(flat_lists.shape[0], -1), flat_lists, num_segments=block_count)
    key_grad = key_grad.reshape(key_blocks.shape).astype(jnp.bfloat16)
    value_grad = value_grad.reshape(value_blocks.shape).astype(jnp.bfloat16)
    return (attended, query_grad, key_grad, value_grad)

def reference(queries, keys, values, out_weight, cotangent, rand_blocks, glob_blocks):
    grad_scale = 1.0 / math.sqrt(DOCS * LEN)

    def split(matrix):
        return matrix.reshape(NB, BLK, H, HS).transpose(2, 0, 1, 3)

    def join(blocks):
        return blocks.transpose(1, 2, 0, 3).reshape(LEN, HD)

    def per_doc(total, items):
        query_doc, key_doc, value_doc, cot_doc, rand_doc, glob_doc = items
        head_cot = jnp.dot(cot_doc, out_weight, preferred_element_type=jnp.float32).astype(jnp.bfloat16)
        lists, live_entries = block_lists(rand_doc, glob_doc, NB)

        def per_head(parts):
            return head_pass(*parts)
        attended, query_grad, key_grad, value_grad = lax.map(per_head, (split(query_doc), split(key_doc), split(value_doc), split(head_cot), lists, live_entries))
        attended = join(attended)
        mixed = jnp.dot(attended, out_weight.T, preferred_element_type=jnp.float32).astype(jnp.bfloat16)
        total = total + jnp.dot(cot_doc.T, attended, preferred_element_type=jnp.float32)
        return (total, (mixed, join(query_grad), join(key_grad), join(value_grad)))
    start_total = jnp.zeros((D_OUT, HD), jnp.float32)
    total, outputs = lax.scan(per_doc, start_total, (queries, keys, values, cotangent, rand_blocks, glob_blocks))
    mixed, grad_queries, grad_keys, grad_values = outputs
    return (mixed, grad_queries, grad_keys, grad_values, total * grad_scale)
```

```python
import math

import jax
import jax.numpy as jnp
from jax import lax
from jax.experimental import pallas as pl
from jax.experimental.pallas import tpu as pltpu
from jax.sharding import Mesh
from jax.sharding import PartitionSpec as P

HS = 128
BLK = 64
NB = 16
LEN = 1024
HD = 2048
SCALE = 1.0 / math.sqrt(HS)
LOG2E = math.log2(math.e)
MASKED = -1e30
CTX = ("xl", "y")
DP = ("z", "xh", "core")
BF = jnp.bfloat16
F32 = jnp.float32
NT = (((1,), (1,)), ((), ()))
NN = (((1,), (0,)), ((), ()))
TN = (((0,), (0,)), ((), ()))


def dot(a, b, dims=NN):
    return lax.dot_general(a, b, dims, preferred_element_type=F32)


def params(mib=48):
    return pltpu.CompilerParams(vmem_limit_bytes=mib * 2**20)


def pack_kernel(q_ref, k_ref, v_ref, out_ref):
    out_ref[0, 0] = q_ref[...]
    out_ref[0, 1] = k_ref[...]
    out_ref[0, 2] = v_ref[...]


def pack_heads(q, k, v):
    spec = pl.BlockSpec((128, 256), lambda c: (0, c))
    return pl.pallas_call(
        pack_kernel,
        grid=(8,),
        in_specs=[spec] * 3,
        out_specs=pl.BlockSpec((1, 3, 128, 256), lambda c: (c, 0, 0, 0)),
        out_shape=jax.ShapeDtypeStruct((8, 3, 128, 256), BF),
        cost_estimate=pl.CostEstimate(flops=0, bytes_accessed=3 * 2**20, transcendentals=0),
        name="pack_heads",
    )(q, k, v)


def halves_kernel(cot_ref, out_ref):
    low = lax.broadcasted_iota(jnp.int32, (128, 128), 1) < 64
    for pair in range(8):
        a = cot_ref[:, 256 * pair : 256 * pair + 128].astype(F32)
        b = cot_ref[:, 256 * pair + 128 : 256 * pair + 256].astype(F32)
        first = jnp.where(low, a, pltpu.roll(b, 64, 1)).astype(BF)
        second = jnp.where(low, pltpu.roll(a, 64, 1), b).astype(BF)
        for y in range(4):
            out_ref[y, :, 128 * pair : 128 * pair + 128] = first
            out_ref[4 + y, :, 128 * pair : 128 * pair + 128] = second


def cot_halves(cot):
    return pl.pallas_call(
        halves_kernel,
        out_shape=jax.ShapeDtypeStruct((8, 128, 1024), BF),
        in_specs=[pl.BlockSpec(memory_space=pltpu.VMEM)],
        out_specs=pl.BlockSpec(memory_space=pltpu.VMEM),
        compiler_params=params(),
        cost_estimate=pl.CostEstimate(flops=0, bytes_accessed=5 * 2**19, transcendentals=0),
        name="cot_halves",
    )(cot)


def live_bias(rand, glob):
    kb = jnp.arange(NB, dtype=jnp.int32)[:, None]
    qb = jnp.arange(NB, dtype=jnp.int32)[None, :]
    live = (jnp.abs(kb - qb) <= 1) | jnp.any(kb[:, :, None] == glob[None, None, :], axis=-1)
    by_rand = jnp.any(rand.transpose(0, 2, 1)[:, :, None, :] == kb[None, None], axis=1)
    bias = jnp.where(live[None] | by_rand, 0.0, MASKED).astype(F32)
    return jnp.repeat(bias, BLK, axis=2)


TILE = 256


def scores_at(k, q, bias):
    s = dot(k, q, NT).reshape(NB, BLK, TILE)
    return s * (SCALE * LOG2E) + bias[:, None, :]


def forward_kernel(qkv_ref, bias_ref, o_ref, stat_ref):
    k = qkv_ref[:, 1].reshape(LEN, HS)
    v_t = qkv_ref[:, 2].reshape(LEN, HS).T
    for t in range(LEN // TILE):
        tok = slice(TILE * t, TILE * t + TILE)
        q = qkv_ref[2 * t : 2 * t + 2, 0].reshape(TILE, HS)
        s = scores_at(k, q, bias_ref[0, :, tok])
        top = jnp.max(s, axis=(0, 1), keepdims=True)
        p = jnp.exp2(s - top)
        total = jnp.sum(p, axis=(0, 1), keepdims=True)
        p_low = (p * (1.0 / total)).astype(BF).reshape(LEN, TILE)
        o_t = dot(v_t, p_low)
        o_ref[tok, :] = o_t.T.astype(BF)
        stat_ref[0, :, tok] = (top + jnp.log2(total))[0]


def forward(qkv, bias):
    return pl.pallas_call(
        forward_kernel,
        grid=(2,),
        in_specs=[
            pl.BlockSpec((8, 3, 128, HS), lambda h: (0, 0, 0, h)),
            pl.BlockSpec((1, NB, LEN), lambda h: (h, 0, 0)),
        ],
        out_specs=[
            pl.BlockSpec((LEN, HS), lambda h: (0, h)),
            pl.BlockSpec((1, 1, LEN), lambda h: (h, 0, 0)),
        ],
        out_shape=[
            jax.ShapeDtypeStruct((LEN, 2 * HS), BF),
            jax.ShapeDtypeStruct((2, 1, LEN), F32),
        ],
        compiler_params=params(),
        cost_estimate=pl.CostEstimate(flops=4 * 2**30, bytes_accessed=2**21, transcendentals=2**21),
        name="attention_forward",
    )(qkv, bias)


def backward_kernel(qkv_ref, bias_ref, stat_ref, o_ref, keep_ref, recv_ref, out_ref, dk_ref, dv_ref):
    k = qkv_ref[:, 1].reshape(LEN, HS)
    v = qkv_ref[:, 2].reshape(LEN, HS)
    k_t = k.T
    for t in range(LEN // TILE):
        tok = slice(TILE * t, TILE * t + TILE)
        q = qkv_ref[2 * t : 2 * t + 2, 0].reshape(TILE, HS)
        do = (keep_ref[tok, :] + recv_ref[tok, :].astype(F32)).astype(BF)
        delta = jnp.sum((do.astype(F32) * o_ref[tok, :].astype(F32)).T, axis=0, keepdims=True)
        p = jnp.exp2(scores_at(k, q, bias_ref[0, :, tok] - stat_ref[0, :, tok]))
        p = p.reshape(LEN, TILE)
        dp = dot(v, do, NT)
        ds = (p * (dp - delta)).astype(BF)
        dq = dot(k_t, ds).T * SCALE
        out_ref[2 * t : 2 * t + 2, 0] = dq.astype(BF).reshape(2, 128, HS)
        dk = dot(ds, q)
        dv = dot(p.astype(BF), do)
        if t == 0:
            dk_ref[...] = dk
            dv_ref[...] = dv
        else:
            dk_ref[...] += dk
            dv_ref[...] += dv
    out_ref[:, 1] = (dk_ref[...] * SCALE).astype(BF).reshape(8, 128, HS)
    out_ref[:, 2] = dv_ref[...].astype(BF).reshape(8, 128, HS)


def backward(qkv, bias, stat, attended, keep, recv):
    wide = pl.BlockSpec((LEN, HS), lambda h: (0, h))
    heads = pl.BlockSpec((8, 3, 128, HS), lambda h: (0, 0, 0, h))
    return pl.pallas_call(
        backward_kernel,
        grid=(2,),
        in_specs=[
            heads,
            pl.BlockSpec((1, NB, LEN), lambda h: (h, 0, 0)),
            pl.BlockSpec((1, 1, LEN), lambda h: (h, 0, 0)),
            wide,
            wide,
            wide,
        ],
        out_specs=heads,
        out_shape=jax.ShapeDtypeStruct((8, 3, 128, 2 * HS), BF),
        scratch_shapes=[pltpu.VMEM((LEN, HS), F32), pltpu.VMEM((LEN, HS), F32)],
        compiler_params=params(),
        cost_estimate=pl.CostEstimate(flops=8 * 2**30, bytes_accessed=2**22, transcendentals=2**21),
        name="attention_backward",
    )(qkv, bias, stat, attended, keep, recv)


def unpack_kernel(in_ref, q_ref, k_ref, v_ref):
    q_ref[...] = in_ref[0, 0]
    k_ref[...] = in_ref[0, 1]
    v_ref[...] = in_ref[0, 2]


def unpack_heads(grads):
    spec = pl.BlockSpec((128, 256), lambda c: (0, c))
    return pl.pallas_call(
        unpack_kernel,
        grid=(8,),
        in_specs=[pl.BlockSpec((1, 3, 128, 256), lambda c: (c, 0, 0, 0))],
        out_specs=[spec] * 3,
        out_shape=[jax.ShapeDtypeStruct((128, HD), BF)] * 3,
        cost_estimate=pl.CostEstimate(flops=0, bytes_accessed=3 * 2**20, transcendentals=0),
        name="unpack_heads",
    )(grads)


def mixed_kernel(in_ref, out_ref):
    low = lax.broadcasted_iota(jnp.int32, (128, 128), 1) < 64
    for pair in range(8):
        cols = slice(128 * pair, 128 * pair + 128)
        first = sum(in_ref[y, :, cols].astype(F32) for y in range(4))
        second = sum(in_ref[4 + y, :, cols].astype(F32) for y in range(4))
        a = jnp.where(low, first, pltpu.roll(second, 64, 1))
        b = jnp.where(low, pltpu.roll(first, 64, 1), second)
        out_ref[:, 256 * pair : 256 * pair + 128] = a.astype(BF)
        out_ref[:, 256 * pair + 128 : 256 * pair + 256] = b.astype(BF)


def finish_mixed(parts):
    return pl.pallas_call(
        mixed_kernel,
        out_shape=jax.ShapeDtypeStruct((128, HD), BF),
        in_specs=[pl.BlockSpec(memory_space=pltpu.VMEM)],
        out_specs=pl.BlockSpec(memory_space=pltpu.VMEM),
        compiler_params=params(),
        cost_estimate=pl.CostEstimate(flops=0, bytes_accessed=5 * 2**19, transcendentals=0),
        name="finish_mixed",
    )(parts)


def ring(size, step):
    return [(i, (i + step) % size) for i in range(size)]


def swap(array):
    return lax.ppermute(array, "xl", ring(2, 1))


def gather_weight(own):
    parts = lax.all_to_all(own, "y", 0, 0, tiled=True).reshape(64, 512)
    core = lax.axis_index("core")
    other = lax.ppermute(parts, "core", ring(2, 1))
    pair = jnp.where(core == 0, jnp.stack([parts, other]), jnp.stack([other, parts]))
    xh = lax.axis_index("xh")
    other = lax.ppermute(pair, "xh", ring(2, 1))
    quad = jnp.where(xh == 0, jnp.stack([pair, other]), jnp.stack([other, pair]))
    z = lax.axis_index("z")
    rel = jnp.stack([quad] + [lax.ppermute(quad, "z", ring(4, step)) for step in (1, 2, 3)])
    at = (z - jnp.arange(4)) % 4
    full = jnp.zeros_like(rel)
    for step in range(4):
        full = lax.dynamic_update_index_in_dim(full, rel[step], at[step], 0)
    return full.reshape(1024, 512)


def on_device(queries, keys, values, out_weight, cotangent, rand_blocks, glob_blocks):
    xl = lax.axis_index("xl")
    sides = out_weight.reshape(16, 2, 1024)
    sides = jnp.where(xl == 0, sides, sides[:, ::-1])
    own = sides.reshape(16, 2, 4, 256).transpose(2, 0, 1, 3).reshape(4, 16, 512)

    qkv = lax.all_to_all(pack_heads(queries[0], keys[0], values[0]), CTX, 0, 0, tiled=True)
    weight = gather_weight(own)
    cot = lax.all_to_all(cot_halves(cotangent[0]), CTX, 0, 0, tiled=True).reshape(LEN, 1024)

    bias = live_bias(rand_blocks[0], glob_blocks[0])
    attended, stat = forward(qkv, bias)
    keep = dot(cot, weight[:, :256])
    recv = swap(dot(cot, weight[:, 256:]).astype(BF))
    other = swap(attended)
    grads = backward(qkv, bias, stat, attended, keep, recv)
    grads = lax.all_to_all(grads, CTX, 0, 0, tiled=True)

    pair = jnp.concatenate([attended, other], axis=1)
    part = dot(pair, weight, NT).astype(BF).reshape(8, 128, 1024)
    part = lax.all_to_all(part, CTX, 0, 0, tiled=True)

    block = dot(cot, pair, TN).astype(BF).reshape(16, 64, 512)
    block = lax.all_to_all(block, DP, 0, 0, tiled=True)
    total_tokens = lax.axis_size(DP) * lax.axis_size(CTX) * cotangent.shape[1]
    rows = jnp.sum(block.astype(F32), axis=0) * (1.0 / math.sqrt(total_tokens))
    rows = lax.all_to_all(rows.reshape(4, 16, 512), "y", 0, 0, tiled=True)
    rows = rows.reshape(4, 16, 2, 256).transpose(1, 2, 0, 3)
    rows = jnp.where(xl == 0, rows, rows[:, ::-1]).reshape(16, HD)

    grad_q, grad_k, grad_v = unpack_heads(grads)
    mixed = finish_mixed(part)
    return (mixed[None], grad_q[None], grad_k[None], grad_v[None], rows)


def solution(mesh):
    fine = Mesh(mesh.devices.reshape(4, 2, 2, 2, 4), ("z", "xh", "core", "xl", "y"))
    tokens = P(DP, CTX, None)
    return jax.shard_map(
        on_device,
        mesh=fine,
        in_specs=(tokens, tokens, tokens, P(DP + CTX, None), tokens, P(DP, CTX, None, None), P(DP, None)),
        out_specs=(tokens, tokens, tokens, tokens, P(DP + CTX, None)),
        check_vma=False,
    )
```

```python
import functools
import math

import jax
import jax.numpy as jnp
from jax import lax
from jax.experimental import pallas as pl
from jax.experimental.pallas import tpu as pltpu
from jax.sharding import Mesh
from jax.sharding import PartitionSpec as P

HS = 128
BLK = 64
NB = 16
LEN = 1024
HD = 2048
SCALE = 1.0 / math.sqrt(HS)
LOG2E = math.log2(math.e)
MASKED = -1e30
CTX = ("xl", "y")
DP = ("z", "xh", "core")
BF = jnp.bfloat16
F32 = jnp.float32
NT = (((1,), (1,)), ((), ()))
NN = (((1,), (0,)), ((), ()))
TN = (((0,), (0,)), ((), ()))


def dot(a, b, dims=NN):
    return lax.dot_general(a, b, dims, preferred_element_type=F32)


def params(mib=48):
    return pltpu.CompilerParams(vmem_limit_bytes=mib * 2**20)


VMEM = pl.BlockSpec(memory_space=pltpu.VMEM)
SMEM = pl.BlockSpec(memory_space=pltpu.SMEM)


def whole(body, name, outs, *args, scalars=0, scratch=(), flops=0):
    one = isinstance(outs[0][0], int)
    made = [jax.ShapeDtypeStruct(*o) for o in ([outs] if one else outs)]
    moved = sum(math.prod(x.shape) * x.dtype.itemsize for x in args)
    moved += sum(math.prod(x.shape) * x.dtype.itemsize for x in made)
    given = pl.pallas_call(
        body,
        in_specs=[SMEM] * scalars + [VMEM] * (len(args) - scalars),
        out_specs=[VMEM] * len(made),
        out_shape=made,
        scratch_shapes=list(scratch),
        compiler_params=params(),
        cost_estimate=pl.CostEstimate(flops=flops, bytes_accessed=moved, transcendentals=0),
        name=name,
    )(*args)
    return given[0] if one else given


def ring(size, step):
    return [(i, (i + step) % size) for i in range(size)]


def swap(array, axis="xl"):
    return lax.ppermute(array, axis, ring(2, 1))


def pack_kernel(q_ref, k_ref, v_ref, out_ref):
    for c in range(8):
        cols = slice(256 * c, 256 * c + 256)
        out_ref[c, 0] = q_ref[:, cols]
        out_ref[c, 1] = k_ref[:, cols]
        out_ref[c, 2] = v_ref[:, cols]


def pack_heads(q, k, v):
    return whole(pack_kernel, "pack_heads", ((8, 3, 128, 256), BF), q, k, v)


def halves_kernel(at_ref, cot_ref, own_ref, other_ref):
    low = lax.broadcasted_iota(jnp.int32, (128, 128), 1) < 64
    mine = at_ref[3] == 0
    for pair in range(8):
        a = cot_ref[:, 256 * pair : 256 * pair + 128].astype(F32)
        b = cot_ref[:, 256 * pair + 128 : 256 * pair + 256].astype(F32)
        first = jnp.where(low, a, pltpu.roll(b, 64, 1))
        second = jnp.where(low, pltpu.roll(a, 64, 1), b)
        cols = slice(128 * pair, 128 * pair + 128)
        own_ref[:, cols] = jnp.where(mine, first, second).astype(BF)
        other_ref[:, cols] = jnp.where(mine, second, first).astype(BF)


def cot_halves(at, cot):
    half = ((128, 1024), BF)
    return whole(halves_kernel, "cot_halves", (half, half), at, cot, scalars=1)


def copies_kernel(at_ref, own_ref, recv_ref, out_ref):
    xl = at_ref[3]
    for y in range(4):
        out_ref[y, xl] = own_ref[...]
        out_ref[y, 1 - xl] = recv_ref[...]


def cot_copies(at, own, recv):
    return whole(copies_kernel, "cot_copies", ((4, 2, 128, 1024), BF), at, own, recv, scalars=1)


def weight_kernel(at_ref, *refs):
    z, xh, core, y = at_ref[0], at_ref[1], at_ref[2], at_ref[4]
    out_ref = refs[-1]
    for step in range(4):
        for h in range(2):
            for k in range(2):
                for b in range(4):
                    zs, ys = lax.rem(z - step + 4, 4), lax.rem(y - b + 4, 4)
                    hs, ks = lax.rem(xh + h, 2), lax.rem(core + k, 2)
                    row = pl.multiple_of(64 * (4 * zs + 2 * hs + ks) + 16 * ys, 16)
                    out_ref[pl.ds(row, 16), :] = refs[step][h, k, b]


def gather_weight(at, own):
    y = at[4]
    parts = [lax.dynamic_index_in_dim(own, y, 0, False)]
    for step in (1, 2, 3):
        piece = lax.dynamic_index_in_dim(own, (y + step) % 4, 0, False)
        parts.append(lax.ppermute(piece, "y", ring(4, step)))
    rows = jnp.stack(parts)
    pair = jnp.stack([rows, swap(rows, "core")])
    quad = jnp.stack([pair, swap(pair, "xh")])
    far = [lax.ppermute(quad, "z", ring(4, step)) for step in (1, 2, 3)]
    return whole(weight_kernel, "place_weight", ((1024, 512), BF), at, quad, *far, scalars=1)


def head_cot_kernel(cot_ref, w_ref, keep_ref, send_ref):
    for y in range(4):
        rows = cot_ref[y].reshape(256, 1024)
        part = dot(rows, w_ref[...])
        for xl in range(2):
            at = slice(128 * (4 * xl + y), 128 * (4 * xl + y) + 128)
            keep_ref[at, :] = part[128 * xl : 128 * xl + 128, :256]
            send_ref[at, :] = part[128 * xl : 128 * xl + 128, 256:].astype(BF)


def head_cot_parts(cot, weight):
    return whole(
        head_cot_kernel, "head_cot", (((LEN, 256), F32), ((LEN, 256), BF)), cot, weight, flops=2**30
    )


def mixed_part_kernel(own_ref, other_ref, w_ref, out_ref):
    for y in range(4):
        for xl in range(2):
            at = slice(128 * (4 * xl + y), 128 * (4 * xl + y) + 128)
            part = dot(own_ref[at, :], w_ref[:, :256], NT) + dot(other_ref[at, :], w_ref[:, 256:], NT)
            out_ref[y, xl] = part.astype(BF)


def mixed_parts(own, other, weight):
    return whole(
        mixed_part_kernel, "mixed_part", ((4, 2, 128, 1024), BF), own, other, weight, flops=2**30
    )


def mixed_sum_kernel(at_ref, in_ref, keep_ref, send_ref):
    xl = at_ref[3]
    keep_ref[...] = sum(in_ref[y, xl].astype(F32) for y in range(4)).astype(BF)
    send_ref[...] = sum(in_ref[y, 1 - xl].astype(F32) for y in range(4)).astype(BF)


def mixed_sum(at, parts):
    half = ((128, 1024), BF)
    return whole(mixed_sum_kernel, "mixed_sum", (half, half), at, parts, scalars=1)


def mixed_join_kernel(at_ref, own_ref, recv_ref, out_ref):
    low = lax.broadcasted_iota(jnp.int32, (128, 128), 1) < 64
    mine = at_ref[3] == 0
    for pair in range(8):
        cols = slice(128 * pair, 128 * pair + 128)
        own, recv = own_ref[:, cols].astype(F32), recv_ref[:, cols].astype(F32)
        first = jnp.where(mine, own, recv)
        second = jnp.where(mine, recv, own)
        out_ref[:, 256 * pair : 256 * pair + 128] = jnp.where(low, first, pltpu.roll(second, 64, 1)).astype(BF)
        out_ref[:, 256 * pair + 128 : 256 * pair + 256] = jnp.where(low, pltpu.roll(first, 64, 1), second).astype(BF)


def mixed_join(at, own, recv):
    return whole(mixed_join_kernel, "mixed_join", ((128, HD), BF), at, own, recv, scalars=1)


def weight_grad_kernel(at_ref, cot_ref, own_ref, other_ref, keep_ref, send_ref, pair_ref, sum_ref):
    core = at_ref[2]
    for y in range(4):
        for xl in range(2):
            at = slice(128 * (4 * xl + y), 128 * (4 * xl + y) + 128)
            to = slice(128 * (2 * y + xl), 128 * (2 * y + xl) + 128)
            pair_ref[to, :256] = own_ref[at, :]
            pair_ref[to, 256:] = other_ref[at, :]
    sum_ref[...] = dot(cot_ref[...].reshape(LEN, 1024), pair_ref[...], TN).reshape(16, 64, 512)
    for d in range(8):
        keep_ref[d] = sum_ref[2 * d + core]
        send_ref[d] = sum_ref[2 * d + 1 - core].astype(BF)


def add_xh_kernel(at_ref, keep_ref, recv_ref, out_ref, send_ref):
    xh = at_ref[1]
    for z in range(4):
        out_ref[z] = keep_ref[2 * z + xh] + recv_ref[2 * z + xh].astype(F32)
        send_ref[z] = (keep_ref[2 * z + 1 - xh] + recv_ref[2 * z + 1 - xh].astype(F32)).astype(BF)


def add_z_kernel(at_ref, keep_ref, recv_ref, out_ref, *send_refs):
    z = at_ref[0]
    out_ref[...] = keep_ref[z] + recv_ref[z].astype(F32)
    for step, ref in enumerate(send_refs, 1):
        to = lax.rem(z + step, 4)
        ref[...] = (keep_ref[to] + recv_ref[to].astype(F32)).astype(BF)


def add_y_kernel(scale, at_ref, own_ref, a_ref, b_ref, c_ref, sum_ref, out_ref, *send_refs):
    y = at_ref[4]
    sum_ref[...] = (own_ref[...] + a_ref[...].astype(F32) + b_ref[...].astype(F32) + c_ref[...].astype(F32)) * scale
    for step, ref in enumerate((out_ref, *send_refs)):
        ref[...] = sum_ref[pl.ds(pl.multiple_of(16 * lax.rem(y + step, 4), 16), 16), :]


def rows_kernel(at_ref, *refs):
    xl, y = at_ref[3], at_ref[4]
    out_ref = refs[-1]
    for step in range(4):
        for side in range(2):
            col = 1024 * lax.rem(xl + side, 2) + 256 * lax.rem(y - step + 4, 4)
            out_ref[:, pl.ds(pl.multiple_of(col, 256), 256)] = refs[step][:, 256 * side : 256 * side + 256]


def weight_grad(at, cot, own, other, scale):
    keep, send = whole(
        weight_grad_kernel,
        "weight_grad",
        (((8, 64, 512), F32), ((8, 64, 512), BF)),
        at,
        cot,
        own,
        other,
        scalars=1,
        scratch=(pltpu.VMEM((LEN, 512), BF), pltpu.VMEM((16, 64, 512), F32)),
        flops=2**30,
    )
    keep, send = whole(
        add_xh_kernel,
        "add_core",
        (((4, 64, 512), F32), ((4, 64, 512), BF)),
        at,
        keep,
        swap(send, "core"),
        scalars=1,
    )
    piece = ((64, 512), BF)
    keep, *sends = whole(
        add_z_kernel,
        "add_xh",
        (((64, 512), F32), piece, piece, piece),
        at,
        keep,
        swap(send, "xh"),
        scalars=1,
    )
    got = [lax.ppermute(send, "z", ring(4, step)) for step, send in enumerate(sends, 1)]
    piece = ((16, 512), F32)
    total, *pieces = whole(
        functools.partial(add_y_kernel, scale),
        "add_z",
        (((64, 512), F32), piece, piece, piece, piece),
        at,
        keep,
        *got,
        scalars=1,
    )
    got = [lax.ppermute(send, "y", ring(4, step)) for step, send in enumerate(pieces[1:], 1)]
    return whole(rows_kernel, "place_rows", ((16, HD), F32), at, pieces[0], *got, scalars=1)


def live_bias(rand, glob):
    kb = jnp.arange(NB, dtype=jnp.int32)[:, None]
    qb = jnp.arange(NB, dtype=jnp.int32)[None, :]
    live = (jnp.abs(kb - qb) <= 1) | jnp.any(kb[:, :, None] == glob[None, None, :], axis=-1)
    by_rand = jnp.any(rand.transpose(0, 2, 1)[:, :, None, :] == kb[None, None], axis=1)
    bias = jnp.where(live[None] | by_rand, 0.0, MASKED).astype(F32)
    return jnp.repeat(bias, BLK, axis=2)


TILE = 256


def scores_at(k, q, bias):
    s = dot(k, q, NT).reshape(NB, BLK, TILE)
    return s * (SCALE * LOG2E) + bias[:, None, :]


def forward_kernel(qkv_ref, bias_ref, o_ref, stat_ref):
    k = qkv_ref[:, 1].reshape(LEN, HS)
    v_t = qkv_ref[:, 2].reshape(LEN, HS).T
    for t in range(LEN // TILE):
        tok = slice(TILE * t, TILE * t + TILE)
        q = qkv_ref[2 * t : 2 * t + 2, 0].reshape(TILE, HS)
        s = scores_at(k, q, bias_ref[0, :, tok])
        top = jnp.max(s, axis=(0, 1), keepdims=True)
        p = jnp.exp2(s - top)
        total = jnp.sum(p, axis=(0, 1), keepdims=True)
        p_low = (p * (1.0 / total)).astype(BF).reshape(LEN, TILE)
        o_t = dot(v_t, p_low)
        o_ref[tok, :] = o_t.T.astype(BF)
        stat_ref[0, :, tok] = (top + jnp.log2(total))[0]


def forward(qkv, bias):
    return pl.pallas_call(
        forward_kernel,
        grid=(2,),
        in_specs=[
            pl.BlockSpec((8, 3, 128, HS), lambda h: (0, 0, 0, h)),
            pl.BlockSpec((1, NB, LEN), lambda h: (h, 0, 0)),
        ],
        out_specs=[
            pl.BlockSpec((LEN, HS), lambda h: (0, h)),
            pl.BlockSpec((1, 1, LEN), lambda h: (h, 0, 0)),
        ],
        out_shape=[
            jax.ShapeDtypeStruct((LEN, 2 * HS), BF),
            jax.ShapeDtypeStruct((2, 1, LEN), F32),
        ],
        compiler_params=params(),
        cost_estimate=pl.CostEstimate(flops=4 * 2**30, bytes_accessed=2**21, transcendentals=2**21),
        name="attention_forward",
    )(qkv, bias)


def backward_kernel(qkv_ref, bias_ref, stat_ref, o_ref, keep_ref, recv_ref, out_ref, dk_ref, dv_ref):
    k = qkv_ref[:, 1].reshape(LEN, HS)
    v = qkv_ref[:, 2].reshape(LEN, HS)
    k_t = k.T
    for t in range(LEN // TILE):
        tok = slice(TILE * t, TILE * t + TILE)
        q = qkv_ref[2 * t : 2 * t + 2, 0].reshape(TILE, HS)
        do = (keep_ref[tok, :] + recv_ref[tok, :].astype(F32)).astype(BF)
        delta = jnp.sum((do.astype(F32) * o_ref[tok, :].astype(F32)).T, axis=0, keepdims=True)
        p = jnp.exp2(scores_at(k, q, bias_ref[0, :, tok] - stat_ref[0, :, tok]))
        p = p.reshape(LEN, TILE)
        dp = dot(v, do, NT)
        ds = (p * (dp - delta)).astype(BF)
        dq = dot(k_t, ds).T * SCALE
        out_ref[2 * t : 2 * t + 2, 0] = dq.astype(BF).reshape(2, 128, HS)
        dk = dot(ds, q)
        dv = dot(p.astype(BF), do)
        if t == 0:
            dk_ref[...] = dk
            dv_ref[...] = dv
        else:
            dk_ref[...] += dk
            dv_ref[...] += dv
    out_ref[:, 1] = (dk_ref[...] * SCALE).astype(BF).reshape(8, 128, HS)
    out_ref[:, 2] = dv_ref[...].astype(BF).reshape(8, 128, HS)


def backward(qkv, bias, stat, attended, keep, recv):
    wide = pl.BlockSpec((LEN, HS), lambda h: (0, h))
    heads = pl.BlockSpec((8, 3, 128, HS), lambda h: (0, 0, 0, h))
    return pl.pallas_call(
        backward_kernel,
        grid=(2,),
        in_specs=[
            heads,
            pl.BlockSpec((1, NB, LEN), lambda h: (h, 0, 0)),
            pl.BlockSpec((1, 1, LEN), lambda h: (h, 0, 0)),
            wide,
            wide,
            wide,
        ],
        out_specs=heads,
        out_shape=jax.ShapeDtypeStruct((8, 3, 128, 2 * HS), BF),
        scratch_shapes=[pltpu.VMEM((LEN, HS), F32), pltpu.VMEM((LEN, HS), F32)],
        compiler_params=params(),
        cost_estimate=pl.CostEstimate(flops=8 * 2**30, bytes_accessed=2**22, transcendentals=2**21),
        name="attention_backward",
    )(qkv, bias, stat, attended, keep, recv)


def unpack_kernel(in_ref, q_ref, k_ref, v_ref):
    for c in range(8):
        cols = slice(256 * c, 256 * c + 256)
        q_ref[:, cols] = in_ref[c, 0]
        k_ref[:, cols] = in_ref[c, 1]
        v_ref[:, cols] = in_ref[c, 2]


def unpack_heads(grads):
    out = ((128, HD), BF)
    return whole(unpack_kernel, "unpack_heads", (out, out, out), grads)


def on_device(queries, keys, values, out_weight, cotangent, rand_blocks, glob_blocks):
    at = jnp.stack([lax.axis_index(name) for name in DP + CTX]).astype(jnp.int32)
    xl = at[3]
    sides = out_weight.reshape(16, 2, 1024)
    sides = jnp.where(xl == 0, sides, sides[:, ::-1])
    own_rows = sides.reshape(16, 2, 4, 256).transpose(2, 0, 1, 3).reshape(4, 16, 512)

    qkv = lax.all_to_all(pack_heads(queries[0], keys[0], values[0]), CTX, 0, 0, tiled=True)
    own, other = cot_halves(at, cotangent[0])
    cot = lax.all_to_all(cot_copies(at, own, swap(other)), "y", 0, 0, tiled=True)
    weight = gather_weight(at, own_rows)

    bias = live_bias(rand_blocks[0], glob_blocks[0])
    attended, stat = forward(qkv, bias)
    attended_other = swap(attended)
    keep, send = head_cot_parts(cot, weight)
    grads = backward(qkv, bias, stat, attended, keep, swap(send))
    grads = lax.all_to_all(grads, CTX, 0, 0, tiled=True)

    part = lax.all_to_all(mixed_parts(attended, attended_other, weight), "y", 0, 0, tiled=True)
    own, other = mixed_sum(at, part)
    mixed = mixed_join(at, own, swap(other))

    total_tokens = lax.axis_size(DP) * lax.axis_size(CTX) * cotangent.shape[1]
    rows = weight_grad(at, cot, attended, attended_other, 1.0 / math.sqrt(total_tokens))

    grad_q, grad_k, grad_v = unpack_heads(grads)
    return (mixed[None], grad_q[None], grad_k[None], grad_v[None], rows)


def solution(mesh):
    fine = Mesh(mesh.devices.reshape(4, 2, 2, 2, 4), ("z", "xh", "core", "xl", "y"))
    tokens = P(DP, CTX, None)
    return jax.shard_map(
        on_device,
        mesh=fine,
        in_specs=(tokens, tokens, tokens, P(DP + CTX, None), tokens, P(DP, CTX, None, None), P(DP, None)),
        out_specs=(tokens, tokens, tokens, tokens, P(DP + CTX, None)),
        check_vma=False,
    )
```

```python
import functools
import math

import jax
import jax.numpy as jnp
from jax import lax
from jax.experimental import pallas as pl
from jax.experimental.pallas import tpu as pltpu
from jax.sharding import Mesh
from jax.sharding import PartitionSpec as P

HS = 128
BLK = 64
NB = 16
LEN = 1024
HD = 2048
SCALE = 1.0 / math.sqrt(HS)
LOG2E = math.log2(math.e)
QKV = 384
ROWS = 416
MASKED = -1e30
CTX = ("xl", "y")
DP = ("z", "xh", "core")
BF = jnp.bfloat16
F32 = jnp.float32
NT = (((1,), (1,)), ((), ()))
NN = (((1,), (0,)), ((), ()))
TN = (((0,), (0,)), ((), ()))


def dot(a, b, dims=NN):
    return lax.dot_general(a, b, dims, preferred_element_type=F32)


def params(mib=48):
    return pltpu.CompilerParams(vmem_limit_bytes=mib * 2**20)


VMEM = pl.BlockSpec(memory_space=pltpu.VMEM)
SMEM = pl.BlockSpec(memory_space=pltpu.SMEM)


HBM = pl.BlockSpec(memory_space=pl.ANY)


def whole(body, name, outs, *args, scalars=0, scratch=(), flops=0, after=()):
    read = len(args)

    def ordered(*refs):
        body(*refs[:read], *refs[read + len(after) :])

    one = isinstance(outs[0][0], int)
    made = [jax.ShapeDtypeStruct(*o) for o in ([outs] if one else outs)]
    moved = sum(math.prod(x.shape) * x.dtype.itemsize for x in args)
    moved += sum(math.prod(x.shape) * x.dtype.itemsize for x in made)
    given = pl.pallas_call(
        ordered,
        in_specs=[SMEM] * scalars + [VMEM] * (len(args) - scalars) + [HBM] * len(after),
        out_specs=[VMEM] * len(made),
        out_shape=made,
        scratch_shapes=list(scratch),
        compiler_params=params(),
        cost_estimate=pl.CostEstimate(flops=1, bytes_accessed=1, transcendentals=0),
        name=name,
    )(*args, *after)
    return given[0] if one else given


def hold(array, after):
    return pl.pallas_call(
        lambda *refs: None,
        in_specs=[HBM] * (1 + len(after)),
        out_specs=HBM,
        out_shape=jax.ShapeDtypeStruct(array.shape, array.dtype),
        input_output_aliases={0: 0},
        cost_estimate=pl.CostEstimate(flops=1, bytes_accessed=1, transcendentals=0),
        name="hold",
    )(array, *after)


def ring(size, step):
    return [(i, (i + step) % size) for i in range(size)]


def swap(array, axis="xl"):
    return lax.ppermute(array, axis, ring(2, 1))


def pack_kernel(q_ref, k_ref, v_ref, out_ref, held_ref, sems):
    copies = []
    for j, ref in enumerate((q_ref, k_ref, v_ref)):
        for half in range(2):
            rows = pl.ds(64 * half, 64)
            copy = pltpu.make_async_copy(ref.at[rows, :], held_ref.at[j, rows, :], sems.at[j, half])
            copy.start()
            copies.append(copy)
    for j in range(3):
        for half in range(2):
            copies[2 * j + half].wait()
            rows = slice(128 * j + 64 * half, 128 * j + 64 * half + 64)
            for c in range(8):
                out_ref[c, rows] = held_ref[j, 64 * half : 64 * half + 64, 256 * c : 256 * c + 256]


def pack_heads(q, k, v):
    return pl.pallas_call(
        pack_kernel,
        in_specs=[pl.BlockSpec(memory_space=pltpu.HBM)] * 3,
        out_specs=VMEM,
        out_shape=jax.ShapeDtypeStruct((8, QKV, 256), BF),
        scratch_shapes=[pltpu.VMEM((3, 128, HD), BF), pltpu.SemaphoreType.DMA((3, 2))],
        compiler_params=params(63),
        cost_estimate=pl.CostEstimate(flops=1, bytes_accessed=1, transcendentals=0),
        name="pack_heads",
    )(q, k, v)


def blocks_kernel(own_ref, out_ref):
    for xh in range(2):
        for xl in range(2):
            for y in range(4):
                for k, side in enumerate((xl, 1 - xl)):
                    cols = slice(1024 * side + 256 * y, 1024 * side + 256 * y + 256)
                    out_ref[8 * xh + 4 * xl + y, :, 256 * k : 256 * k + 256] = own_ref[:, cols]


def near_kernel(at_ref, *refs):
    out_ref = refs[-1]
    for step in range(4):
        out_ref[lax.rem(at_ref[0] - step + 4, 4)] = refs[step][...]


def weight_kernel(at_ref, own_ref, other_ref, out_ref):
    core = at_ref[2]
    for z in range(4):
        for h in range(2):
            out_ref[4 * z + 2 * h + core] = own_ref[z, h]
            out_ref[4 * z + 2 * h + 1 - core] = other_ref[z, h]


def gather_weight(at, own):
    blocks = whole(blocks_kernel, "weight_blocks", ((16, 16, 512), BF), own)
    rows = lax.all_to_all(blocks, ("xh",) + CTX, 0, 0, tiled=True).reshape(2, 128, 512)
    far = [lax.ppermute(rows, "z", ring(4, step)) for step in (1, 2, 3)]
    near = whole(near_kernel, "place_z", ((4, 2, 128, 512), BF), at, rows, *far, scalars=1)
    full = whole(weight_kernel, "place_core", ((16, 128, 512), BF), at, near, swap(near, "core"), scalars=1)
    return full.reshape(HD, 512), rows


def gather_cot(own):
    back = lax.ppermute(own, "y", ring(4, 1))
    on = lax.ppermute(own, "y", ring(4, 3))
    return own, back, on, lax.ppermute(back[:64], "y", ring(4, 1)), lax.ppermute(on[64:], "y", ring(4, 3))


def place_cot(y, full_ref, own_ref, back_ref, on_ref, far_0_ref, far_1_ref):
    full_ref[y] = own_ref[...]
    full_ref[lax.rem(y + 3, 4)] = back_ref[...]
    full_ref[lax.rem(y + 1, 4)] = on_ref[...]
    full_ref[lax.rem(y + 2, 4), :64] = far_0_ref[...]
    full_ref[lax.rem(y + 2, 4), 64:] = far_1_ref[...]


def head_cot_kernel(at_ref, *refs):
    cot_refs, (w_ref, keep_ref, send_ref, full_ref) = refs[:5], refs[5:]
    place_cot(at_ref[4], full_ref, *cot_refs)
    for t in range(2):
        rows = slice(256 * t, 256 * t + 256)
        both = dot(full_ref[2 * t : 2 * t + 2].reshape(256, HD), w_ref[...]).astype(BF)
        keep_ref[rows, :] = both[:, :256]
        send_ref[rows, :] = both[:, 256:]


def head_cot_parts(at, cot, weight):
    half = ((512, 256), BF)
    full = pltpu.VMEM((4, 128, HD), BF)
    return whole(head_cot_kernel, "head_cot", (half, half), at, *cot, weight, scalars=1, scratch=(full,))


def mixed_part_kernel(at_ref, own_ref, other_ref, w_ref, out_ref):
    for y in range(4):
        own = own_ref[pl.ds(pl.multiple_of(512 * at_ref[3] + 128 * y, 128), 128), :]
        other = other_ref[128 * y : 128 * y + 128, :]
        for n in range(4):
            outs = slice(512 * n, 512 * n + 512)
            part = dot(own, w_ref[outs, :256], NT) + dot(other, w_ref[outs, 256:], NT)
            out_ref[y, :, outs] = part.astype(BF)


def mixed_parts(at, own, other, weight):
    return whole(mixed_part_kernel, "mixed_part", ((4, 128, HD), BF), at, own, other, weight, scalars=1)


def mixed_kernel(in_ref, out_ref):
    out_ref[...] = sum(in_ref[y].astype(F32) for y in range(4)).astype(BF)


def finish_mixed(parts):
    return whole(mixed_kernel, "finish_mixed", ((128, HD), BF), parts)


def weight_grad_kernel(at_ref, *refs):
    cot_refs, (own_ref, other_ref, keep_ref, send_ref, full_ref, pair_ref, sum_ref) = refs[:5], refs[5:]
    core, xl = at_ref[2], at_ref[3]
    place_cot(at_ref[4], full_ref, *cot_refs)
    pair_ref[:, :256] = own_ref[pl.ds(pl.multiple_of(512 * xl, 512), 512), :]
    pair_ref[:, 256:] = other_ref[...]
    for z in range(4):
        cot = full_ref[:, :, 512 * z : 512 * z + 512].reshape(512, 512)
        sum_ref[...] = dot(cot, pair_ref[...], TN).reshape(4, 128, 512)
        for h in range(2):
            keep_ref[z, h] = sum_ref[2 * h + core]
            send_ref[z, h] = sum_ref[2 * h + 1 - core].astype(BF)


def add_core_kernel(at_ref, keep_ref, recv_ref, out_ref, *send_refs):
    z = at_ref[0]
    out_ref[...] = keep_ref[z] + recv_ref[z].astype(F32)
    for step, ref in enumerate(send_refs, 1):
        to = lax.rem(z + step, 4)
        ref[...] = (keep_ref[to] + recv_ref[to].astype(F32)).astype(BF)


def add_z_kernel(at_ref, own_ref, a_ref, b_ref, c_ref, out_ref, send_ref):
    xh = at_ref[1]

    def total(h):
        return own_ref[h] + a_ref[h].astype(F32) + b_ref[h].astype(F32) + c_ref[h].astype(F32)

    out_ref[...] = total(xh)
    send_ref[...] = total(1 - xh).astype(BF)


def attach_kernel(scale, keep_ref, recv_ref, grads_ref, out_ref):
    total = ((keep_ref[...] + recv_ref[...].astype(F32)) * scale).astype(BF)
    for c in range(8):
        rows = slice(16 * c, 16 * c + 16)
        out_ref[c, :QKV] = grads_ref[c]
        out_ref[c, QKV : QKV + 16] = total[rows, :256]
        out_ref[c, QKV + 16 :] = total[rows, 256:]


def attach(keep, recv, grads, scale):
    body = functools.partial(attach_kernel, scale)
    return whole(body, "attach", ((8, ROWS, 256), BF), keep, recv, grads)


def weight_grad(at, cot, own, other, after):
    shape = (4, 2, 128, 512)
    keep, send = whole(
        weight_grad_kernel,
        "weight_grad",
        ((shape, F32), (shape, BF)),
        at,
        *cot,
        own,
        other,
        scalars=1,
        after=after,
        scratch=(pltpu.VMEM((4, 128, HD), BF), pltpu.VMEM((512, 512), BF), pltpu.VMEM((4, 128, 512), F32)),
    )
    two, one = ((2, 128, 512), BF), ((128, 512), BF)
    keep, *sends = whole(
        add_core_kernel, "add_core", ((two[0], F32), two, two, two), at, keep, swap(send, "core"), scalars=1
    )
    started = sends[-1]
    got = [lax.ppermute(send, "z", ring(4, step)) for step, send in enumerate(sends, 1)]
    keep, send = whole(add_z_kernel, "add_z", ((one[0], F32), one), at, keep, *got, scalars=1)
    return started, keep, swap(send, "xh")


def live_bias(rand, glob):
    kb = jnp.arange(NB, dtype=jnp.int32)[:, None]
    qb = jnp.arange(NB, dtype=jnp.int32)[None, :]
    live = (jnp.abs(kb - qb) <= 1) | jnp.any(kb[:, :, None] == glob[None, None, :], axis=-1)
    by_rand = jnp.any(rand.transpose(0, 2, 1)[:, :, None, :] == kb[None, None], axis=1)
    bias = jnp.where(live[None] | by_rand, 0.0, MASKED).astype(F32)
    return jnp.repeat(bias, BLK, axis=2)


TILE = 256


def scores_at(k, q, bias):
    s = dot(k, q, NT).reshape(NB, BLK, TILE)
    return s * (SCALE * LOG2E) + bias[:, None, :]


def forward_kernel(qkv_ref, bias_ref, o_ref, stat_ref):
    k = qkv_ref[:, 128:256].reshape(LEN, HS)
    v_t = qkv_ref[:, 256:384].reshape(LEN, HS).T
    for t in range(LEN // TILE):
        tok = slice(TILE * t, TILE * t + TILE)
        q = qkv_ref[2 * t : 2 * t + 2, :128].reshape(TILE, HS)
        s = scores_at(k, q, bias_ref[0, :, tok])
        top = jnp.max(s, axis=(0, 1), keepdims=True)
        p = jnp.exp2(s - top)
        total = jnp.sum(p, axis=(0, 1), keepdims=True)
        p_low = (p * (1.0 / total)).astype(BF).reshape(LEN, TILE)
        o_t = dot(v_t, p_low)
        o_ref[tok, :] = o_t.T.astype(BF)
        stat_ref[0, :, tok] = (top + jnp.log2(total))[0]


def forward(qkv, bias):
    return pl.pallas_call(
        forward_kernel,
        grid=(2,),
        in_specs=[
            pl.BlockSpec((8, QKV, HS), lambda h: (0, 0, h)),
            pl.BlockSpec((1, NB, LEN), lambda h: (h, 0, 0)),
        ],
        out_specs=[
            pl.BlockSpec((LEN, HS), lambda h: (0, h)),
            pl.BlockSpec((1, 1, LEN), lambda h: (h, 0, 0)),
        ],
        out_shape=[
            jax.ShapeDtypeStruct((LEN, 2 * HS), BF),
            jax.ShapeDtypeStruct((2, 1, LEN), F32),
        ],
        compiler_params=params(),
        cost_estimate=pl.CostEstimate(flops=1, bytes_accessed=1, transcendentals=0),
        name="attention_forward",
    )(qkv, bias)


def backward_kernel(at_ref, qkv_ref, bias_ref, stat_ref, o_ref, keep_ref, recv_ref, *refs):
    out_ref, dk_ref, dv_ref = refs[-3:]
    k = qkv_ref[:, 128:256].reshape(LEN, HS)
    v = qkv_ref[:, 256:384].reshape(LEN, HS)
    k_t = k.T
    for t in range(LEN // TILE):
        tok = slice(TILE * t, TILE * t + TILE)
        q = qkv_ref[2 * t : 2 * t + 2, :128].reshape(TILE, HS)
        half, part = divmod(TILE * t, 512)
        part = slice(part, part + TILE)
        do = jnp.where(at_ref[3] == half, keep_ref[part, :], recv_ref[part, :])
        delta = jnp.sum((do.astype(F32) * o_ref[tok, :].astype(F32)).T, axis=0, keepdims=True)
        p = jnp.exp2(scores_at(k, q, bias_ref[0, :, tok] - stat_ref[0, :, tok]))
        p = p.reshape(LEN, TILE)
        dp = dot(v, do, NT)
        ds = (p * (dp - delta)).astype(BF)
        dq = dot(k_t, ds).T * SCALE
        out_ref[2 * t : 2 * t + 2, :128] = dq.astype(BF).reshape(2, 128, HS)
        dk = dot(ds, q)
        dv = dot(p.astype(BF), do)
        if t == 0:
            dk_ref[...] = dk
            dv_ref[...] = dv
        else:
            dk_ref[...] += dk
            dv_ref[...] += dv
    out_ref[:, 128:256] = (dk_ref[...] * SCALE).astype(BF).reshape(8, 128, HS)
    out_ref[:, 256:384] = dv_ref[...].astype(BF).reshape(8, 128, HS)


def backward(at, qkv, bias, stat, attended, keep, recv, after):
    wide = pl.BlockSpec((LEN, HS), lambda h: (0, h))
    half = pl.BlockSpec((512, HS), lambda h: (0, h))
    heads = pl.BlockSpec((8, QKV, HS), lambda h: (0, 0, h))
    return pl.pallas_call(
        backward_kernel,
        grid=(2,),
        in_specs=[
            SMEM,
            heads,
            pl.BlockSpec((1, NB, LEN), lambda h: (h, 0, 0)),
            pl.BlockSpec((1, 1, LEN), lambda h: (h, 0, 0)),
            wide,
            half,
            half,
            *[HBM] * len(after),
        ],
        out_specs=heads,
        out_shape=jax.ShapeDtypeStruct((8, QKV, 2 * HS), BF),
        scratch_shapes=[pltpu.VMEM((LEN, HS), F32), pltpu.VMEM((LEN, HS), F32)],
        compiler_params=params(),
        cost_estimate=pl.CostEstimate(flops=1, bytes_accessed=1, transcendentals=0),
        name="attention_backward",
    )(at, qkv, bias, stat, attended, keep, recv, *after)


def unpack_kernel(in_ref, q_ref, k_ref, v_ref, rows_ref):
    for c in range(8):
        cols = slice(256 * c, 256 * c + 256)
        for j, ref in enumerate((q_ref, k_ref, v_ref)):
            ref[:, cols] = in_ref[c, 128 * j : 128 * j + 128]
    for side in range(2):
        for y in range(4):
            first = in_ref[4 * side + y, QKV : QKV + 16].astype(F32)
            second = in_ref[4 * (1 - side) + y, QKV + 16 :].astype(F32)
            rows_ref[:, 1024 * side + 256 * y : 1024 * side + 256 * y + 256] = first + second


def unpack_heads(grads):
    out = ((128, HD), BF)
    return whole(unpack_kernel, "unpack_heads", (out, out, out, ((16, HD), F32)), grads)


def on_device(queries, keys, values, out_weight, cotangent, rand_blocks, glob_blocks):
    at = jnp.stack([lax.axis_index(name) for name in DP + CTX]).astype(jnp.int32)
    xl = at[3]
    cot = gather_cot(cotangent[0])
    weight, early = gather_weight(at, out_weight)
    qkv = hold(pack_heads(queries[0], keys[0], values[0]), (early,))
    qkv = lax.all_to_all(qkv, CTX, 0, 0, tiled=True)

    bias = live_bias(rand_blocks[0], glob_blocks[0])
    attended, stat = forward(qkv, bias)
    other = swap(lax.dynamic_slice(attended, (512 * (1 - xl), 0), (512, 256)))
    keep, send = head_cot_parts(at, cot, weight)
    part = mixed_parts(at, attended, other, weight)
    started, rows, rows_recv = weight_grad(at, cot, attended, other, (part,))
    part = lax.all_to_all(part, "y", 0, 0, tiled=True)
    grads = backward(at, qkv, bias, stat, attended, keep, swap(send), (started,))
    total_tokens = lax.axis_size(DP) * lax.axis_size(CTX) * cotangent.shape[1]
    grads = attach(rows, rows_recv, grads, 1.0 / math.sqrt(total_tokens))
    grads = lax.all_to_all(grads, CTX, 0, 0, tiled=True)

    mixed = finish_mixed(part)
    grad_q, grad_k, grad_v, grad_w = unpack_heads(grads)
    return (mixed[None], grad_q[None], grad_k[None], grad_v[None], grad_w)


def solution(mesh):
    fine = Mesh(mesh.devices.reshape(4, 2, 2, 2, 4), ("z", "xh", "core", "xl", "y"))
    tokens = P(DP, CTX, None)
    return jax.shard_map(
        on_device,
        mesh=fine,
        in_specs=(tokens, tokens, tokens, P(DP + CTX, None), tokens, P(DP, CTX, None, None), P(DP, None)),
        out_specs=(tokens, tokens, tokens, tokens, P(DP + CTX, None)),
        check_vma=False,
    )
```

```python
import functools
import math

import jax
import jax.numpy as jnp
from jax import lax
from jax.experimental import pallas as pl
from jax.experimental.pallas import tpu as pltpu
from jax.sharding import Mesh
from jax.sharding import PartitionSpec as P

HS = 128
BLK = 64
NB = 16
LEN = 1024
HD = 2048
SCALE = 1.0 / math.sqrt(HS)
LOG2E = math.log2(math.e)
QKV = 384
ROWS = 416
MASKED = -1e30
CTX = ("xl", "y")
DP = ("z", "xh", "core")
BF = jnp.bfloat16
F32 = jnp.float32
NT = (((1,), (1,)), ((), ()))
NN = (((1,), (0,)), ((), ()))
TN = (((0,), (0,)), ((), ()))


def dot(a, b, dims=NN):
    return lax.dot_general(a, b, dims, preferred_element_type=F32)


def params(mib=48):
    return pltpu.CompilerParams(vmem_limit_bytes=mib * 2**20)


VMEM = pl.BlockSpec(memory_space=pltpu.VMEM)
SMEM = pl.BlockSpec(memory_space=pltpu.SMEM)


HBM = pl.BlockSpec(memory_space=pl.ANY)


def whole(body, name, outs, *args, scalars=0, scratch=(), flops=0, after=()):
    read = len(args)

    def ordered(*refs):
        body(*refs[:read], *refs[read + len(after) :])

    one = isinstance(outs[0][0], int)
    made = [jax.ShapeDtypeStruct(*o) for o in ([outs] if one else outs)]
    moved = sum(math.prod(x.shape) * x.dtype.itemsize for x in args)
    moved += sum(math.prod(x.shape) * x.dtype.itemsize for x in made)
    given = pl.pallas_call(
        ordered,
        in_specs=[SMEM] * scalars + [VMEM] * (len(args) - scalars) + [HBM] * len(after),
        out_specs=[VMEM] * len(made),
        out_shape=made,
        scratch_shapes=list(scratch),
        compiler_params=params(),
        cost_estimate=pl.CostEstimate(flops=1, bytes_accessed=1, transcendentals=0),
        name=name,
    )(*args, *after)
    return given[0] if one else given


def hold(array, after):
    return pl.pallas_call(
        lambda *refs: None,
        in_specs=[HBM] * (1 + len(after)),
        out_specs=HBM,
        out_shape=jax.ShapeDtypeStruct(array.shape, array.dtype),
        input_output_aliases={0: 0},
        cost_estimate=pl.CostEstimate(flops=1, bytes_accessed=1, transcendentals=0),
        name="hold",
    )(array, *after)


def ring(size, step):
    return [(i, (i + step) % size) for i in range(size)]


def swap(array, axis="xl"):
    return lax.ppermute(array, axis, ring(2, 1))


def pack_kernel(q_ref, k_ref, v_ref, out_ref, held_ref, sems):
    copies = []
    for j, ref in enumerate((q_ref, k_ref, v_ref)):
        for half in range(2):
            rows = pl.ds(64 * half, 64)
            copy = pltpu.make_async_copy(ref.at[rows, :], held_ref.at[j, rows, :], sems.at[j, half])
            copy.start()
            copies.append(copy)
    for j in range(3):
        for half in range(2):
            copies[2 * j + half].wait()
            rows = slice(128 * j + 64 * half, 128 * j + 64 * half + 64)
            for c in range(8):
                out_ref[c, rows] = held_ref[j, 64 * half : 64 * half + 64, 256 * c : 256 * c + 256]


def pack_heads(q, k, v):
    return pl.pallas_call(
        pack_kernel,
        in_specs=[pl.BlockSpec(memory_space=pltpu.HBM)] * 3,
        out_specs=VMEM,
        out_shape=jax.ShapeDtypeStruct((8, QKV, 256), BF),
        scratch_shapes=[pltpu.VMEM((3, 128, HD), BF), pltpu.SemaphoreType.DMA((3, 2))],
        compiler_params=params(63),
        cost_estimate=pl.CostEstimate(flops=1, bytes_accessed=1, transcendentals=0),
        name="pack_heads",
    )(q, k, v)


def blocks_kernel(own_ref, out_ref):
    for xh in range(2):
        for xl in range(2):
            for y in range(4):
                for k, side in enumerate((xl, 1 - xl)):
                    cols = slice(1024 * side + 256 * y, 1024 * side + 256 * y + 256)
                    out_ref[8 * xh + 4 * xl + y, :, 256 * k : 256 * k + 256] = own_ref[:, cols]


def near_kernel(at_ref, *refs):
    out_ref = refs[-1]
    for step in range(4):
        out_ref[lax.rem(at_ref[0] - step + 4, 4)] = refs[step][...]


def weight_kernel(at_ref, own_ref, other_ref, out_ref):
    core = at_ref[2]
    for z in range(4):
        for h in range(2):
            out_ref[4 * z + 2 * h + core] = own_ref[z, h]
            out_ref[4 * z + 2 * h + 1 - core] = other_ref[z, h]


def gather_weight(at, own):
    blocks = whole(blocks_kernel, "weight_blocks", ((16, 16, 512), BF), own)
    rows = lax.all_to_all(blocks, ("xh",) + CTX, 0, 0, tiled=True).reshape(2, 128, 512)
    far = [lax.ppermute(rows, "z", ring(4, step)) for step in (1, 2, 3)]
    near = whole(near_kernel, "place_z", ((4, 2, 128, 512), BF), at, rows, *far, scalars=1)
    full = whole(weight_kernel, "place_core", ((16, 128, 512), BF), at, near, swap(near, "core"), scalars=1)
    return full.reshape(HD, 512), rows


def near_cot(own):
    return own, lax.ppermute(own, "y", ring(4, 1)), lax.ppermute(own, "y", ring(4, 3))


def relay_kernel(back_ref, on_ref, first_ref, last_ref):
    first_ref[...] = back_ref[:64]
    last_ref[...] = on_ref[64:]


def far_cot(back, on, after):
    half = ((64, HD), BF)
    first, last = whole(relay_kernel, "cot_relay", (half, half), back, on, after=after)
    return lax.ppermute(first, "y", ring(4, 1)), lax.ppermute(last, "y", ring(4, 3))


def place_cot(y, full_ref, own_ref, back_ref, on_ref, far_0_ref, far_1_ref):
    full_ref[y] = own_ref[...]
    full_ref[lax.rem(y + 3, 4)] = back_ref[...]
    full_ref[lax.rem(y + 1, 4)] = on_ref[...]
    full_ref[lax.rem(y + 2, 4), :64] = far_0_ref[...]
    full_ref[lax.rem(y + 2, 4), 64:] = far_1_ref[...]


def head_cot_kernel(at_ref, *refs):
    cot_refs, (w_ref, keep_ref, send_ref, full_ref) = refs[:5], refs[5:]
    place_cot(at_ref[4], full_ref, *cot_refs)
    both = dot(full_ref[...].reshape(512, HD), w_ref[...]).astype(BF)
    keep_ref[...] = both[:, :256]
    send_ref[...] = both[:, 256:]


def head_cot_parts(at, cot, weight, after):
    half = ((512, 256), BF)
    full = pltpu.VMEM((4, 128, HD), BF)
    return whole(head_cot_kernel, "head_cot", (half, half), at, *cot, weight, scalars=1, after=after, scratch=(full,))


def mixed_part_kernel(at_ref, own_ref, other_ref, w_ref, out_ref, pair_ref):
    pair_ref[:, :256] = own_ref[pl.ds(pl.multiple_of(512 * at_ref[3], 512), 512), :]
    pair_ref[:, 256:] = other_ref[...]
    for n in range(4):
        outs = slice(512 * n, 512 * n + 512)
        out_ref[:, :, outs] = dot(pair_ref[...], w_ref[outs, :], NT).astype(BF).reshape(4, 128, 512)


def mixed_parts(at, own, other, weight, after):
    return whole(
        mixed_part_kernel,
        "mixed_part",
        ((4, 128, HD), BF),
        at,
        own,
        other,
        weight,
        scalars=1,
        after=after,
        scratch=(pltpu.VMEM((512, 512), BF),),
    )


def mixed_kernel(in_ref, out_ref):
    out_ref[...] = sum(in_ref[y].astype(F32) for y in range(4)).astype(BF)


def finish_mixed(parts):
    return whole(mixed_kernel, "finish_mixed", ((128, HD), BF), parts)


def weight_grad_kernel(at_ref, *refs):
    cot_refs, (own_ref, other_ref, keep_ref, send_ref, full_ref, pair_ref, sum_ref) = refs[:5], refs[5:]
    core, xl = at_ref[2], at_ref[3]
    place_cot(at_ref[4], full_ref, *cot_refs)
    pair_ref[:, :256] = own_ref[pl.ds(pl.multiple_of(512 * xl, 512), 512), :]
    pair_ref[:, 256:] = other_ref[...]
    for z in range(4):
        cot = full_ref[:, :, 512 * z : 512 * z + 512].reshape(512, 512)
        sum_ref[...] = dot(cot, pair_ref[...], TN).reshape(4, 128, 512)
        for h in range(2):
            keep_ref[z, h] = sum_ref[2 * h + core].astype(BF)
            send_ref[z, h] = sum_ref[2 * h + 1 - core].astype(BF)


def add_core_kernel(at_ref, keep_ref, recv_ref, out_ref, *send_refs):
    z = at_ref[0]
    out_ref[...] = keep_ref[z].astype(F32) + recv_ref[z].astype(F32)
    for step, ref in enumerate(send_refs, 1):
        to = lax.rem(z + step, 4)
        ref[...] = (keep_ref[to].astype(F32) + recv_ref[to].astype(F32)).astype(BF)


def add_z_kernel(at_ref, own_ref, a_ref, b_ref, c_ref, out_ref, send_ref):
    xh = at_ref[1]

    def total(h):
        return own_ref[h] + a_ref[h].astype(F32) + b_ref[h].astype(F32) + c_ref[h].astype(F32)

    out_ref[...] = total(xh)
    send_ref[...] = total(1 - xh).astype(BF)


def attach_kernel(scale, keep_ref, recv_ref, grads_ref, out_ref):
    total = ((keep_ref[...] + recv_ref[...].astype(F32)) * scale).astype(BF)
    for c in range(8):
        rows = slice(16 * c, 16 * c + 16)
        out_ref[c, :QKV] = grads_ref[c]
        out_ref[c, QKV : QKV + 16] = total[rows, :256]
        out_ref[c, QKV + 16 :] = total[rows, 256:]


def attach(keep, recv, grads, scale):
    body = functools.partial(attach_kernel, scale)
    return whole(body, "attach", ((8, ROWS, 256), BF), keep, recv, grads)


def weight_grad(at, cot, own, other, after):
    shape = (4, 2, 128, 512)
    keep, send = whole(
        weight_grad_kernel,
        "weight_grad",
        ((shape, BF), (shape, BF)),
        at,
        *cot,
        own,
        other,
        scalars=1,
        after=after,
        scratch=(pltpu.VMEM((4, 128, HD), BF), pltpu.VMEM((512, 512), BF), pltpu.VMEM((4, 128, 512), F32)),
    )
    first, two = send, ((2, 128, 512), BF)
    keep, *sends = whole(
        add_core_kernel, "add_core", ((two[0], F32), two, two, two), at, keep, swap(send, "core"), scalars=1
    )
    return keep, [lax.ppermute(send, "z", ring(4, step)) for step, send in enumerate(sends, 1)], sends[-1], first


def sum_z(at, keep, got, after):
    one = ((128, 512), BF)
    keep, send = whole(
        add_z_kernel, "add_z", ((one[0], F32), one), at, keep, *got, scalars=1, after=after
    )
    return keep, swap(send, "xh")


def live_bias(rand, glob):
    kb = jnp.arange(NB, dtype=jnp.int32)[:, None]
    qb = jnp.arange(NB, dtype=jnp.int32)[None, :]
    live = (jnp.abs(kb - qb) <= 1) | jnp.any(kb[:, :, None] == glob[None, None, :], axis=-1)
    by_rand = jnp.any(rand.transpose(0, 2, 1)[:, :, None, :] == kb[None, None], axis=1)
    bias = jnp.where(live[None] | by_rand, 0.0, MASKED).astype(F32)
    return jnp.repeat(bias, BLK, axis=2)


TILE = 256


def scores_at(k, q, bias):
    s = dot(k, q, NT).reshape(NB, BLK, TILE)
    return s * (SCALE * LOG2E) + bias[:, None, :]


def forward_kernel(qkv_ref, bias_ref, *refs):
    o_ref, stat_ref = refs[-2:]
    k = qkv_ref[:, 128:256].reshape(LEN, HS)
    v_t = qkv_ref[:, 256:384].reshape(LEN, HS).T
    for t in range(LEN // TILE):
        tok = slice(TILE * t, TILE * t + TILE)
        q = qkv_ref[2 * t : 2 * t + 2, :128].reshape(TILE, HS)
        s = scores_at(k, q, bias_ref[0, :, tok])
        top = jnp.max(s, axis=(0, 1), keepdims=True)
        p = jnp.exp2(s - top)
        total = jnp.sum(p, axis=(0, 1), keepdims=True)
        o_t = dot(v_t, p.astype(BF).reshape(LEN, TILE)) * (1.0 / total[0])
        o_ref[tok, :] = o_t.T.astype(BF)
        stat_ref[0, :, tok] = (top + jnp.log2(total))[0]


def forward(qkv, bias, after):
    return pl.pallas_call(
        forward_kernel,
        grid=(2,),
        in_specs=[
            pl.BlockSpec((8, QKV, HS), lambda h: (0, 0, h)),
            pl.BlockSpec((1, NB, LEN), lambda h: (h, 0, 0)),
            *[HBM] * len(after),
        ],
        out_specs=[
            pl.BlockSpec((LEN, HS), lambda h: (0, h)),
            pl.BlockSpec((1, 1, LEN), lambda h: (h, 0, 0)),
        ],
        out_shape=[
            jax.ShapeDtypeStruct((LEN, 2 * HS), BF),
            jax.ShapeDtypeStruct((2, 1, LEN), F32),
        ],
        compiler_params=params(),
        cost_estimate=pl.CostEstimate(flops=9 * 10**9, bytes_accessed=1, transcendentals=0),
        name="attention_forward",
    )(qkv, bias, *after)


def backward_kernel(at_ref, qkv_ref, bias_ref, stat_ref, o_ref, keep_ref, recv_ref, *refs):
    out_ref, dk_ref, dv_ref = refs[-3:]
    k = qkv_ref[:, 128:256].reshape(LEN, HS)
    v = qkv_ref[:, 256:384].reshape(LEN, HS)
    k_t = k.T
    for t in range(LEN // TILE):
        tok = slice(TILE * t, TILE * t + TILE)
        q = qkv_ref[2 * t : 2 * t + 2, :128].reshape(TILE, HS)
        half, part = divmod(TILE * t, 512)
        part = slice(part, part + TILE)
        do = jnp.where(at_ref[3] == half, keep_ref[part, :], recv_ref[part, :])
        delta = jnp.sum((do.astype(F32) * o_ref[tok, :].astype(F32)).T, axis=0, keepdims=True)
        p = jnp.exp2(scores_at(k, q, bias_ref[0, :, tok] - stat_ref[0, :, tok]))
        p = p.reshape(LEN, TILE)
        dp = dot(v, do, NT)
        ds = (p * (dp - delta)).astype(BF)
        dq = dot(k_t, ds).T * SCALE
        out_ref[2 * t : 2 * t + 2, :128] = dq.astype(BF).reshape(2, 128, HS)
        dk = dot(ds, q)
        dv = dot(p.astype(BF), do)
        if t == 0:
            dk_ref[...] = dk
            dv_ref[...] = dv
        else:
            dk_ref[...] += dk
            dv_ref[...] += dv
    out_ref[:, 128:256] = (dk_ref[...] * SCALE).astype(BF).reshape(8, 128, HS)
    out_ref[:, 256:384] = dv_ref[...].astype(BF).reshape(8, 128, HS)


def backward(at, qkv, bias, stat, attended, keep, recv, after):
    wide = pl.BlockSpec((LEN, HS), lambda h: (0, h))
    half = pl.BlockSpec((512, HS), lambda h: (0, h))
    heads = pl.BlockSpec((8, QKV, HS), lambda h: (0, 0, h))
    return pl.pallas_call(
        backward_kernel,
        grid=(2,),
        in_specs=[
            SMEM,
            heads,
            pl.BlockSpec((1, NB, LEN), lambda h: (h, 0, 0)),
            pl.BlockSpec((1, 1, LEN), lambda h: (h, 0, 0)),
            wide,
            half,
            half,
            *[HBM] * len(after),
        ],
        out_specs=heads,
        out_shape=jax.ShapeDtypeStruct((8, QKV, 2 * HS), BF),
        scratch_shapes=[pltpu.VMEM((LEN, HS), F32), pltpu.VMEM((LEN, HS), F32)],
        compiler_params=params(),
        cost_estimate=pl.CostEstimate(flops=1, bytes_accessed=1, transcendentals=0),
        name="attention_backward",
    )(at, qkv, bias, stat, attended, keep, recv, *after)


def unpack_kernel(in_ref, q_ref, k_ref, v_ref, rows_ref):
    for c in range(8):
        cols = slice(256 * c, 256 * c + 256)
        for j, ref in enumerate((q_ref, k_ref, v_ref)):
            ref[:, cols] = in_ref[c, 128 * j : 128 * j + 128]
    for side in range(2):
        for y in range(4):
            first = in_ref[4 * side + y, QKV : QKV + 16].astype(F32)
            second = in_ref[4 * (1 - side) + y, QKV + 16 :].astype(F32)
            rows_ref[:, 1024 * side + 256 * y : 1024 * side + 256 * y + 256] = first + second


def unpack_heads(grads):
    out = ((128, HD), BF)
    return whole(unpack_kernel, "unpack_heads", (out, out, out, ((16, HD), F32)), grads)


def on_device(queries, keys, values, out_weight, cotangent, rand_blocks, glob_blocks):
    at = jnp.stack([lax.axis_index(name) for name in DP + CTX]).astype(jnp.int32)
    xl = at[3]
    cot = near_cot(cotangent[0])
    weight, early = gather_weight(at, out_weight)
    qkv = hold(pack_heads(queries[0], keys[0], values[0]), (early,))
    qkv = lax.all_to_all(qkv, CTX, 0, 0, tiled=True)

    bias = live_bias(rand_blocks[0], glob_blocks[0])
    attended, stat = forward(qkv, bias, ())
    cot += far_cot(cot[1], cot[2], (stat,))
    other = swap(lax.dynamic_slice(attended, (512 * (1 - xl), 0), (512, 256)))
    part = mixed_parts(at, attended, other, weight, ())
    rows, got, started, first = weight_grad(at, cot, attended, other, (part,))
    keep, send = head_cot_parts(at, cot, weight, (first,))
    part = lax.all_to_all(part, "y", 0, 0, tiled=True)
    grads = backward(at, qkv, bias, stat, attended, keep, swap(send), (started,))
    rows, rows_recv = sum_z(at, rows, got, (grads,))
    total_tokens = lax.axis_size(DP) * lax.axis_size(CTX) * cotangent.shape[1]
    grads = attach(rows, rows_recv, grads, 1.0 / math.sqrt(total_tokens))
    grads = lax.all_to_all(grads, CTX, 0, 0, tiled=True)

    mixed = finish_mixed(part)
    grad_q, grad_k, grad_v, grad_w = unpack_heads(grads)
    return (mixed[None], grad_q[None], grad_k[None], grad_v[None], grad_w)


def solution(mesh):
    fine = Mesh(mesh.devices.reshape(4, 2, 2, 2, 4), ("z", "xh", "core", "xl", "y"))
    tokens = P(DP, CTX, None)
    return jax.shard_map(
        on_device,
        mesh=fine,
        in_specs=(tokens, tokens, tokens, P(DP + CTX, None), tokens, P(DP, CTX, None, None), P(DP, None)),
        out_specs=(tokens, tokens, tokens, tokens, P(DP + CTX, None)),
        check_vma=False,
    )
```

```python
import functools
import math

import jax
import jax.numpy as jnp
from jax import lax
from jax.experimental import pallas as pl
from jax.experimental.pallas import tpu as pltpu
from jax.sharding import Mesh
from jax.sharding import PartitionSpec as P

HS = 128
BLK = 64
NB = 16
LEN = 1024
HD = 2048
SCALE = 1.0 / math.sqrt(HS)
LOG2E = math.log2(math.e)
QKV = 384
ROWS = 416
MASKED = -1e30
CTX = ("xl", "y")
DP = ("z", "xh", "core")
BF = jnp.bfloat16
F32 = jnp.float32
NT = (((1,), (1,)), ((), ()))
NN = (((1,), (0,)), ((), ()))
TN = (((0,), (0,)), ((), ()))


def dot(a, b, dims=NN):
    return lax.dot_general(a, b, dims, preferred_element_type=F32)


def params(mib=48):
    return pltpu.CompilerParams(vmem_limit_bytes=mib * 2**20)


VMEM = pl.BlockSpec(memory_space=pltpu.VMEM)
SMEM = pl.BlockSpec(memory_space=pltpu.SMEM)


HBM = pl.BlockSpec(memory_space=pl.ANY)


def whole(body, name, outs, *args, scalars=0, scratch=(), flops=0, after=()):
    read = len(args)

    def ordered(*refs):
        body(*refs[:read], *refs[read + len(after) :])

    one = isinstance(outs[0][0], int)
    made = [jax.ShapeDtypeStruct(*o) for o in ([outs] if one else outs)]
    moved = sum(math.prod(x.shape) * x.dtype.itemsize for x in args)
    moved += sum(math.prod(x.shape) * x.dtype.itemsize for x in made)
    given = pl.pallas_call(
        ordered,
        in_specs=[SMEM] * scalars + [VMEM] * (len(args) - scalars) + [HBM] * len(after),
        out_specs=[VMEM] * len(made),
        out_shape=made,
        scratch_shapes=list(scratch),
        compiler_params=params(),
        cost_estimate=pl.CostEstimate(flops=1, bytes_accessed=1, transcendentals=0),
        name=name,
    )(*args, *after)
    return given[0] if one else given


def hold(array, after):
    return pl.pallas_call(
        lambda *refs: None,
        in_specs=[HBM] * (1 + len(after)),
        out_specs=HBM,
        out_shape=jax.ShapeDtypeStruct(array.shape, array.dtype),
        input_output_aliases={0: 0},
        cost_estimate=pl.CostEstimate(flops=1, bytes_accessed=1, transcendentals=0),
        name="hold",
    )(array, *after)


def ring(size, step):
    return [(i, (i + step) % size) for i in range(size)]


def swap(array, axis="xl"):
    return lax.ppermute(array, axis, ring(2, 1))


def pack_kernel(q_ref, k_ref, v_ref, out_ref, held_ref, sems):
    copies = []
    for j, ref in enumerate((q_ref, k_ref, v_ref)):
        for half in range(2):
            rows = pl.ds(64 * half, 64)
            copy = pltpu.make_async_copy(ref.at[rows, :], held_ref.at[j, rows, :], sems.at[j, half])
            copy.start()
            copies.append(copy)
    for j in range(3):
        for half in range(2):
            copies[2 * j + half].wait()
            rows = slice(128 * j + 64 * half, 128 * j + 64 * half + 64)
            for c in range(8):
                out_ref[c, rows] = held_ref[j, 64 * half : 64 * half + 64, 256 * c : 256 * c + 256]


def pack_heads(q, k, v):
    return pl.pallas_call(
        pack_kernel,
        in_specs=[pl.BlockSpec(memory_space=pltpu.HBM)] * 3,
        out_specs=VMEM,
        out_shape=jax.ShapeDtypeStruct((8, QKV, 256), BF),
        scratch_shapes=[pltpu.VMEM((3, 128, HD), BF), pltpu.SemaphoreType.DMA((3, 2))],
        compiler_params=params(63),
        cost_estimate=pl.CostEstimate(flops=1, bytes_accessed=1, transcendentals=0),
        name="pack_heads",
    )(q, k, v)


def blocks_kernel(own_ref, out_ref):
    for xh in range(2):
        for xl in range(2):
            for y in range(4):
                for k, side in enumerate((xl, 1 - xl)):
                    cols = slice(1024 * side + 256 * y, 1024 * side + 256 * y + 256)
                    out_ref[8 * xh + 4 * xl + y, :, 256 * k : 256 * k + 256] = own_ref[:, cols]


def near_kernel(at_ref, *refs):
    out_ref = refs[-1]
    for step in range(4):
        out_ref[lax.rem(at_ref[0] - step + 4, 4)] = refs[step][...]


def weight_kernel(at_ref, own_ref, other_ref, out_ref):
    core = at_ref[2]
    for z in range(4):
        for h in range(2):
            out_ref[4 * z + 2 * h + core] = own_ref[z, h]
            out_ref[4 * z + 2 * h + 1 - core] = other_ref[z, h]


def gather_weight(at, own):
    blocks = whole(blocks_kernel, "weight_blocks", ((16, 16, 512), BF), own)
    rows = lax.all_to_all(blocks, ("xh",) + CTX, 0, 0, tiled=True).reshape(2, 128, 512)
    far = [lax.ppermute(rows, "z", ring(4, step)) for step in (1, 2, 3)]
    near = whole(near_kernel, "place_z", ((4, 2, 128, 512), BF), at, rows, *far, scalars=1)
    full = whole(weight_kernel, "place_core", ((16, 128, 512), BF), at, near, swap(near, "core"), scalars=1)
    return full.reshape(HD, 512), rows


def near_cot(own):
    return own, lax.ppermute(own, "y", ring(4, 1)), lax.ppermute(own, "y", ring(4, 3))


def relay_kernel(back_ref, on_ref, first_ref, last_ref):
    first_ref[...] = back_ref[:64]
    last_ref[...] = on_ref[64:]


def far_cot(back, on, after):
    half = ((64, HD), BF)
    first, last = whole(relay_kernel, "cot_relay", (half, half), back, on, after=after)
    return lax.ppermute(first, "y", ring(4, 1)), lax.ppermute(last, "y", ring(4, 3))


def place_cot(y, full_ref, own_ref, back_ref, on_ref, far_0_ref, far_1_ref):
    full_ref[y] = own_ref[...]
    full_ref[lax.rem(y + 3, 4)] = back_ref[...]
    full_ref[lax.rem(y + 1, 4)] = on_ref[...]
    full_ref[lax.rem(y + 2, 4), :64] = far_0_ref[...]
    full_ref[lax.rem(y + 2, 4), 64:] = far_1_ref[...]


def head_cot_kernel(at_ref, *refs):
    cot_refs, (w_ref, keep_ref, send_ref, full_ref) = refs[:5], refs[5:]
    place_cot(at_ref[4], full_ref, *cot_refs)
    both = dot(full_ref[...].reshape(512, HD), w_ref[...]).astype(BF)
    keep_ref[...] = both[:, :256]
    send_ref[...] = both[:, 256:]


def head_cot_parts(at, cot, weight, after):
    half = ((512, 256), BF)
    full = pltpu.VMEM((4, 128, HD), BF)
    return whole(head_cot_kernel, "head_cot", (half, half), at, *cot, weight, scalars=1, after=after, scratch=(full,))


def mixed_part_kernel(at_ref, own_ref, other_ref, w_ref, out_ref, pair_ref):
    pair_ref[:, :256] = own_ref[pl.ds(pl.multiple_of(512 * at_ref[3], 512), 512), :]
    pair_ref[:, 256:] = other_ref[...]
    for n in range(4):
        outs = slice(512 * n, 512 * n + 512)
        out_ref[:, :, outs] = dot(pair_ref[...], w_ref[outs, :], NT).astype(BF).reshape(4, 128, 512)


def mixed_parts(at, own, other, weight, after):
    return whole(
        mixed_part_kernel,
        "mixed_part",
        ((4, 128, HD), BF),
        at,
        own,
        other,
        weight,
        scalars=1,
        after=after,
        scratch=(pltpu.VMEM((512, 512), BF),),
    )


def mixed_kernel(in_ref, out_ref):
    out_ref[...] = sum(in_ref[y].astype(F32) for y in range(4)).astype(BF)


def finish_mixed(parts):
    return whole(mixed_kernel, "finish_mixed", ((128, HD), BF), parts)


def weight_grad_kernel(at_ref, *refs):
    cot_refs, (own_ref, other_ref, keep_ref, send_ref, full_ref, pair_ref, sum_ref) = refs[:5], refs[5:]
    core, xl = at_ref[2], at_ref[3]
    place_cot(at_ref[4], full_ref, *cot_refs)
    pair_ref[:, :256] = own_ref[pl.ds(pl.multiple_of(512 * xl, 512), 512), :]
    pair_ref[:, 256:] = other_ref[...]
    for z in range(4):
        cot = full_ref[:, :, 512 * z : 512 * z + 512].reshape(512, 512)
        sum_ref[...] = dot(cot, pair_ref[...], TN).reshape(4, 128, 512)
        for h in range(2):
            keep_ref[z, h] = sum_ref[2 * h + core].astype(BF)
            send_ref[z, h] = sum_ref[2 * h + 1 - core].astype(BF)


def add_core_kernel(at_ref, keep_ref, recv_ref, out_ref, *send_refs):
    z = at_ref[0]
    out_ref[...] = keep_ref[z].astype(F32) + recv_ref[z].astype(F32)
    for step, ref in enumerate(send_refs, 1):
        to = lax.rem(z + step, 4)
        ref[...] = (keep_ref[to].astype(F32) + recv_ref[to].astype(F32)).astype(BF)


def add_z_kernel(at_ref, own_ref, a_ref, b_ref, c_ref, out_ref, send_ref):
    xh = at_ref[1]

    def total(h):
        return own_ref[h] + a_ref[h].astype(F32) + b_ref[h].astype(F32) + c_ref[h].astype(F32)

    out_ref[...] = total(xh)
    send_ref[...] = total(1 - xh).astype(BF)


def attach_kernel(scale, keep_ref, recv_ref, grads_ref, out_ref):
    total = ((keep_ref[...] + recv_ref[...].astype(F32)) * scale).astype(BF)
    for c in range(8):
        rows = slice(16 * c, 16 * c + 16)
        out_ref[c, :QKV] = grads_ref[c]
        out_ref[c, QKV : QKV + 16] = total[rows, :256]
        out_ref[c, QKV + 16 :] = total[rows, 256:]


def attach(keep, recv, grads, scale):
    body = functools.partial(attach_kernel, scale)
    return whole(body, "attach", ((8, ROWS, 256), BF), keep, recv, grads)


def weight_grad(at, cot, own, other, after):
    shape = (4, 2, 128, 512)
    keep, send = whole(
        weight_grad_kernel,
        "weight_grad",
        ((shape, BF), (shape, BF)),
        at,
        *cot,
        own,
        other,
        scalars=1,
        after=after,
        scratch=(pltpu.VMEM((4, 128, HD), BF), pltpu.VMEM((512, 512), BF), pltpu.VMEM((4, 128, 512), F32)),
    )
    first, two = send, ((2, 128, 512), BF)
    keep, *sends = whole(
        add_core_kernel, "add_core", ((two[0], F32), two, two, two), at, keep, swap(send, "core"), scalars=1
    )
    return keep, [lax.ppermute(send, "z", ring(4, step)) for step, send in enumerate(sends, 1)], sends[-1], first


def sum_z(at, keep, got, after):
    one = ((128, 512), BF)
    keep, send = whole(
        add_z_kernel, "add_z", ((one[0], F32), one), at, keep, *got, scalars=1, after=after
    )
    return keep, swap(send, "xh")


def live_bias(rand, glob):
    kb = jnp.arange(NB, dtype=jnp.int32)[:, None]
    qb = jnp.arange(NB, dtype=jnp.int32)[None, :]
    live = (jnp.abs(kb - qb) <= 1) | jnp.any(kb[:, :, None] == glob[None, None, :], axis=-1)
    by_rand = jnp.any(rand.transpose(0, 2, 1)[:, :, None, :] == kb[None, None], axis=1)
    bias = jnp.where(live[None] | by_rand, 0.0, MASKED).astype(F32)
    return jnp.repeat(bias, BLK, axis=2)


TILE = 512
STEP = TILE // 128


def scores_at(k, q, bias):
    s = dot(k, q, NT).reshape(NB, BLK, TILE)
    return s * (SCALE * LOG2E) + bias[:, None, :]


def forward_kernel(qkv_ref, bias_ref, *refs):
    o_ref, stat_ref = refs[-2:]
    k = qkv_ref[:, 128:256].reshape(LEN, HS)
    v_t = qkv_ref[:, 256:384].reshape(LEN, HS).T
    for t in range(LEN // TILE):
        tok = slice(TILE * t, TILE * t + TILE)
        q = qkv_ref[STEP * t : STEP * t + STEP, :128].reshape(TILE, HS)
        s = scores_at(k, q, bias_ref[0, :, tok])
        top = jnp.max(s, axis=(0, 1), keepdims=True)
        p = jnp.exp2(s - top)
        total = jnp.sum(p, axis=(0, 1), keepdims=True)
        o_t = dot(v_t, p.astype(BF).reshape(LEN, TILE)) * (1.0 / total[0])
        o_ref[tok, :] = o_t.T.astype(BF)
        stat_ref[0, :, tok] = (top + jnp.log2(total))[0]


def forward(qkv, bias, after):
    return pl.pallas_call(
        forward_kernel,
        grid=(2,),
        in_specs=[
            pl.BlockSpec((8, QKV, HS), lambda h: (0, 0, h)),
            pl.BlockSpec((1, NB, LEN), lambda h: (h, 0, 0)),
            *[HBM] * len(after),
        ],
        out_specs=[
            pl.BlockSpec((LEN, HS), lambda h: (0, h)),
            pl.BlockSpec((1, 1, LEN), lambda h: (h, 0, 0)),
        ],
        out_shape=[
            jax.ShapeDtypeStruct((LEN, 2 * HS), BF),
            jax.ShapeDtypeStruct((2, 1, LEN), F32),
        ],
        compiler_params=params(),
        cost_estimate=pl.CostEstimate(flops=9 * 10**9, bytes_accessed=1, transcendentals=0),
        name="attention_forward",
    )(qkv, bias, *after)


def backward_kernel(at_ref, qkv_ref, bias_ref, stat_ref, o_ref, keep_ref, recv_ref, *refs):
    out_ref, dk_ref, dv_ref = refs[-3:]
    k = qkv_ref[:, 128:256].reshape(LEN, HS)
    v = qkv_ref[:, 256:384].reshape(LEN, HS)
    k_t = k.T
    for t in range(LEN // TILE):
        tok = slice(TILE * t, TILE * t + TILE)
        q = qkv_ref[STEP * t : STEP * t + STEP, :128].reshape(TILE, HS)
        half, part = divmod(TILE * t, 512)
        part = slice(part, part + TILE)
        do = jnp.where(at_ref[3] == half, keep_ref[part, :], recv_ref[part, :])
        delta = jnp.sum((do.astype(F32) * o_ref[tok, :].astype(F32)).T, axis=0, keepdims=True)
        p = jnp.exp2(scores_at(k, q, bias_ref[0, :, tok] - stat_ref[0, :, tok]))
        p = p.reshape(LEN, TILE)
        dp = dot(v, do, NT)
        ds = (p * (dp - delta)).astype(BF)
        dq = dot(k_t, ds).T * SCALE
        out_ref[STEP * t : STEP * t + STEP, :128] = dq.astype(BF).reshape(STEP, 128, HS)
        dk = dot(ds, q)
        dv = dot(p.astype(BF), do)
        if t == 0:
            dk_ref[...] = dk
            dv_ref[...] = dv
        else:
            dk_ref[...] += dk
            dv_ref[...] += dv
    out_ref[:, 128:256] = (dk_ref[...] * SCALE).astype(BF).reshape(8, 128, HS)
    out_ref[:, 256:384] = dv_ref[...].astype(BF).reshape(8, 128, HS)


def backward(at, qkv, bias, stat, attended, keep, recv, after):
    wide = pl.BlockSpec((LEN, HS), lambda h: (0, h))
    half = pl.BlockSpec((512, HS), lambda h: (0, h))
    heads = pl.BlockSpec((8, QKV, HS), lambda h: (0, 0, h))
    return pl.pallas_call(
        backward_kernel,
        grid=(2,),
        in_specs=[
            SMEM,
            heads,
            pl.BlockSpec((1, NB, LEN), lambda h: (h, 0, 0)),
            pl.BlockSpec((1, 1, LEN), lambda h: (h, 0, 0)),
            wide,
            half,
            half,
            *[HBM] * len(after),
        ],
        out_specs=heads,
        out_shape=jax.ShapeDtypeStruct((8, QKV, 2 * HS), BF),
        scratch_shapes=[pltpu.VMEM((LEN, HS), F32), pltpu.VMEM((LEN, HS), F32)],
        compiler_params=params(),
        cost_estimate=pl.CostEstimate(flops=1, bytes_accessed=1, transcendentals=0),
        name="attention_backward",
    )(at, qkv, bias, stat, attended, keep, recv, *after)


def unpack_kernel(in_ref, q_ref, k_ref, v_ref, rows_ref):
    for c in range(8):
        cols = slice(256 * c, 256 * c + 256)
        for j, ref in enumerate((q_ref, k_ref, v_ref)):
            ref[:, cols] = in_ref[c, 128 * j : 128 * j + 128]
    for side in range(2):
        for y in range(4):
            first = in_ref[4 * side + y, QKV : QKV + 16].astype(F32)
            second = in_ref[4 * (1 - side) + y, QKV + 16 :].astype(F32)
            rows_ref[:, 1024 * side + 256 * y : 1024 * side + 256 * y + 256] = first + second


def unpack_heads(grads):
    out = ((128, HD), BF)
    return whole(unpack_kernel, "unpack_heads", (out, out, out, ((16, HD), F32)), grads)


def on_device(queries, keys, values, out_weight, cotangent, rand_blocks, glob_blocks):
    at = jnp.stack([lax.axis_index(name) for name in DP + CTX]).astype(jnp.int32)
    xl = at[3]
    cot = near_cot(cotangent[0])
    weight, early = gather_weight(at, out_weight)
    qkv = hold(pack_heads(queries[0], keys[0], values[0]), (early, *cot[1:3]))
    qkv = lax.all_to_all(qkv, CTX, 0, 0, tiled=True)

    bias = live_bias(rand_blocks[0], glob_blocks[0])
    attended, stat = forward(qkv, bias, ())
    cot += far_cot(cot[1], cot[2], (stat,))
    other = swap(lax.dynamic_slice(attended, (512 * (1 - xl), 0), (512, 256)))
    part = mixed_parts(at, attended, other, weight, ())
    rows, got, started, first = weight_grad(at, cot, attended, other, (part,))
    keep, send = head_cot_parts(at, cot, weight, (first,))
    part = lax.all_to_all(part, "y", 0, 0, tiled=True)
    grads = backward(at, qkv, bias, stat, attended, keep, swap(send), (started,))
    rows, rows_recv = sum_z(at, rows, got, (grads,))
    total_tokens = lax.axis_size(DP) * lax.axis_size(CTX) * cotangent.shape[1]
    grads = attach(rows, rows_recv, grads, 1.0 / math.sqrt(total_tokens))
    grads = lax.all_to_all(grads, CTX, 0, 0, tiled=True)

    mixed = finish_mixed(part)
    grad_q, grad_k, grad_v, grad_w = unpack_heads(grads)
    return (mixed[None], grad_q[None], grad_k[None], grad_v[None], grad_w)


def solution(mesh):
    fine = Mesh(mesh.devices.reshape(4, 2, 2, 2, 4), ("z", "xh", "core", "xl", "y"))
    tokens = P(DP, CTX, None)
    return jax.shard_map(
        on_device,
        mesh=fine,
        in_specs=(tokens, tokens, tokens, P(DP + CTX, None), tokens, P(DP, CTX, None, None), P(DP, None)),
        out_specs=(tokens, tokens, tokens, tokens, P(DP + CTX, None)),
        check_vma=False,
    )
```

```python
import functools
import math

import jax
import jax.numpy as jnp
from jax import lax
from jax.experimental import pallas as pl
from jax.experimental.pallas import tpu as pltpu
from jax.sharding import Mesh
from jax.sharding import PartitionSpec as P

HS = 128
BLK = 64
NB = 16
LEN = 1024
HD = 2048
SCALE = 1.0 / math.sqrt(HS)
LOG2E = math.log2(math.e)
QKV = 384
ROWS = 416
MASKED = -1e30
CTX = ("xl", "y")
DP = ("z", "xh", "core")
Z_STEPS = (2, 1, 3)
BF = jnp.bfloat16
F32 = jnp.float32
NT = (((1,), (1,)), ((), ()))
NN = (((1,), (0,)), ((), ()))
TN = (((0,), (0,)), ((), ()))


def dot(a, b, dims=NN):
    return lax.dot_general(a, b, dims, preferred_element_type=F32)


def params(mib=48):
    return pltpu.CompilerParams(vmem_limit_bytes=mib * 2**20)


VMEM = pl.BlockSpec(memory_space=pltpu.VMEM)
SMEM = pl.BlockSpec(memory_space=pltpu.SMEM)


HBM = pl.BlockSpec(memory_space=pl.ANY)


def whole(body, name, outs, *args, scalars=0, scratch=(), flops=0, after=()):
    read = len(args)

    def ordered(*refs):
        body(*refs[:read], *refs[read + len(after) :])

    one = isinstance(outs[0][0], int)
    made = [jax.ShapeDtypeStruct(*o) for o in ([outs] if one else outs)]
    moved = sum(math.prod(x.shape) * x.dtype.itemsize for x in args)
    moved += sum(math.prod(x.shape) * x.dtype.itemsize for x in made)
    given = pl.pallas_call(
        ordered,
        in_specs=[SMEM] * scalars + [VMEM] * (len(args) - scalars) + [HBM] * len(after),
        out_specs=[VMEM] * len(made),
        out_shape=made,
        scratch_shapes=list(scratch),
        compiler_params=params(),
        cost_estimate=pl.CostEstimate(flops=1, bytes_accessed=1, transcendentals=0),
        name=name,
    )(*args, *after)
    return given[0] if one else given


def hold(array, after):
    return pl.pallas_call(
        lambda *refs: None,
        in_specs=[HBM] * (1 + len(after)),
        out_specs=HBM,
        out_shape=jax.ShapeDtypeStruct(array.shape, array.dtype),
        input_output_aliases={0: 0},
        cost_estimate=pl.CostEstimate(flops=1, bytes_accessed=1, transcendentals=0),
        name="hold",
    )(array, *after)


def ring(size, step):
    return [(i, (i + step) % size) for i in range(size)]


def swap(array, axis="xl"):
    return lax.ppermute(array, axis, ring(2, 1))


def pack_kernel(q_ref, k_ref, v_ref, out_ref, held_ref, sems):
    copies = []
    for j, ref in enumerate((q_ref, k_ref, v_ref)):
        for half in range(2):
            rows = pl.ds(64 * half, 64)
            copy = pltpu.make_async_copy(ref.at[rows, :], held_ref.at[j, rows, :], sems.at[j, half])
            copy.start()
            copies.append(copy)
    for j in range(3):
        for half in range(2):
            copies[2 * j + half].wait()
            rows = slice(128 * j + 64 * half, 128 * j + 64 * half + 64)
            for c in range(8):
                out_ref[c, rows] = held_ref[j, 64 * half : 64 * half + 64, 256 * c : 256 * c + 256]


def pack_heads(q, k, v):
    return pl.pallas_call(
        pack_kernel,
        in_specs=[pl.BlockSpec(memory_space=pltpu.HBM)] * 3,
        out_specs=VMEM,
        out_shape=jax.ShapeDtypeStruct((8, QKV, 256), BF),
        scratch_shapes=[pltpu.VMEM((3, 128, HD), BF), pltpu.SemaphoreType.DMA((3, 2))],
        compiler_params=params(63),
        cost_estimate=pl.CostEstimate(flops=1, bytes_accessed=1, transcendentals=0),
        name="pack_heads",
    )(q, k, v)


def blocks_kernel(own_ref, out_ref):
    for xh in range(2):
        for xl in range(2):
            for y in range(4):
                for k, side in enumerate((xl, 1 - xl)):
                    cols = slice(1024 * side + 256 * y, 1024 * side + 256 * y + 256)
                    out_ref[8 * xh + 4 * xl + y, :, 256 * k : 256 * k + 256] = own_ref[:, cols]


def near_kernel(at_ref, *refs):
    out_ref = refs[-1]
    for step in range(4):
        out_ref[lax.rem(at_ref[0] - step + 4, 4)] = refs[step][...]


def weight_kernel(at_ref, own_ref, other_ref, out_ref):
    core = at_ref[2]
    for z in range(4):
        for h in range(2):
            out_ref[4 * z + 2 * h + core] = own_ref[z, h]
            out_ref[4 * z + 2 * h + 1 - core] = other_ref[z, h]


def gather_weight(at, own):
    blocks = whole(blocks_kernel, "weight_blocks", ((16, 16, 512), BF), own)
    rows = lax.all_to_all(blocks, ("xh",) + CTX, 0, 0, tiled=True).reshape(2, 128, 512)
    far = [lax.ppermute(rows, "z", ring(4, step)) for step in (1, 2, 3)]
    near = whole(near_kernel, "place_z", ((4, 2, 128, 512), BF), at, rows, *far, scalars=1)
    full = whole(weight_kernel, "place_core", ((16, 128, 512), BF), at, near, swap(near, "core"), scalars=1)
    return full.reshape(HD, 512), rows


def near_cot(own):
    return own, lax.ppermute(own, "y", ring(4, 1)), lax.ppermute(own, "y", ring(4, 3))


def relay_kernel(back_ref, on_ref, first_ref, last_ref):
    first_ref[...] = back_ref[:64]
    last_ref[...] = on_ref[64:]


def far_cot(back, on, after):
    half = ((64, HD), BF)
    first, last = whole(relay_kernel, "cot_relay", (half, half), back, on, after=after)
    return lax.ppermute(first, "y", ring(4, 1)), lax.ppermute(last, "y", ring(4, 3))


def place_cot(y, full_ref, own_ref, back_ref, on_ref, far_0_ref, far_1_ref):
    full_ref[y] = own_ref[...]
    full_ref[lax.rem(y + 3, 4)] = back_ref[...]
    full_ref[lax.rem(y + 1, 4)] = on_ref[...]
    full_ref[lax.rem(y + 2, 4), :64] = far_0_ref[...]
    full_ref[lax.rem(y + 2, 4), 64:] = far_1_ref[...]


def head_cot_kernel(at_ref, *refs):
    cot_refs, (w_ref, keep_ref, send_ref, full_ref) = refs[:5], refs[5:]
    place_cot(at_ref[4], full_ref, *cot_refs)
    both = dot(full_ref[...].reshape(512, HD), w_ref[...]).astype(BF)
    keep_ref[...] = both[:, :256]
    send_ref[...] = both[:, 256:]


def head_cot_parts(at, cot, weight, after):
    half = ((512, 256), BF)
    full = pltpu.VMEM((4, 128, HD), BF)
    return whole(head_cot_kernel, "head_cot", (half, half), at, *cot, weight, scalars=1, after=after, scratch=(full,))


def mixed_part_kernel(at_ref, own_ref, other_ref, w_ref, out_ref, pair_ref):
    pair_ref[:, :256] = own_ref[pl.ds(pl.multiple_of(512 * at_ref[3], 512), 512), :]
    pair_ref[:, 256:] = other_ref[...]
    for n in range(4):
        outs = slice(512 * n, 512 * n + 512)
        out_ref[:, :, outs] = dot(pair_ref[...], w_ref[outs, :], NT).astype(BF).reshape(4, 128, 512)


def mixed_parts(at, own, other, weight, after):
    return whole(
        mixed_part_kernel,
        "mixed_part",
        ((4, 128, HD), BF),
        at,
        own,
        other,
        weight,
        scalars=1,
        after=after,
        scratch=(pltpu.VMEM((512, 512), BF),),
    )


def mixed_kernel(in_ref, out_ref):
    out_ref[...] = sum(in_ref[y].astype(F32) for y in range(4)).astype(BF)


def finish_mixed(parts):
    return whole(mixed_kernel, "finish_mixed", ((128, HD), BF), parts)


def weight_grad_kernel(at_ref, *refs):
    cot_refs, (own_ref, other_ref, keep_ref, send_ref, full_ref, pair_ref, sum_ref) = refs[:5], refs[5:]
    core, xl = at_ref[2], at_ref[3]
    place_cot(at_ref[4], full_ref, *cot_refs)
    pair_ref[:, :256] = own_ref[pl.ds(pl.multiple_of(512 * xl, 512), 512), :]
    pair_ref[:, 256:] = other_ref[...]
    for z in range(4):
        cot = full_ref[:, :, 512 * z : 512 * z + 512].reshape(512, 512)
        sum_ref[...] = dot(cot, pair_ref[...], TN).reshape(4, 128, 512)
        for h in range(2):
            keep_ref[z, h] = sum_ref[2 * h + core].astype(BF)
            send_ref[z, h] = sum_ref[2 * h + 1 - core].astype(BF)


def add_core_kernel(at_ref, keep_ref, recv_ref, out_ref, *send_refs):
    z = at_ref[0]
    out_ref[...] = keep_ref[z].astype(F32) + recv_ref[z].astype(F32)
    for step, ref in zip(Z_STEPS, send_refs):
        to = lax.rem(z + step, 4)
        ref[...] = (keep_ref[to].astype(F32) + recv_ref[to].astype(F32)).astype(BF)


def add_z_kernel(at_ref, own_ref, a_ref, b_ref, c_ref, out_ref, send_ref):
    xh = at_ref[1]

    def total(h):
        return own_ref[h] + a_ref[h].astype(F32) + b_ref[h].astype(F32) + c_ref[h].astype(F32)

    out_ref[...] = total(xh)
    send_ref[...] = total(1 - xh).astype(BF)


def attach_kernel(scale, keep_ref, recv_ref, grads_ref, out_ref):
    total = ((keep_ref[...] + recv_ref[...].astype(F32)) * scale).astype(BF)
    for c in range(8):
        rows = slice(16 * c, 16 * c + 16)
        out_ref[c, :QKV] = grads_ref[c]
        out_ref[c, QKV : QKV + 16] = total[rows, :256]
        out_ref[c, QKV + 16 :] = total[rows, 256:]


def attach(keep, recv, grads, scale):
    body = functools.partial(attach_kernel, scale)
    return whole(body, "attach", ((8, ROWS, 256), BF), keep, recv, grads)


def weight_grad(at, cot, own, other, after):
    shape = (4, 2, 128, 512)
    keep, send = whole(
        weight_grad_kernel,
        "weight_grad",
        ((shape, BF), (shape, BF)),
        at,
        *cot,
        own,
        other,
        scalars=1,
        after=after,
        scratch=(pltpu.VMEM((4, 128, HD), BF), pltpu.VMEM((512, 512), BF), pltpu.VMEM((4, 128, 512), F32)),
    )
    first, two = send, ((2, 128, 512), BF)
    keep, *sends = whole(
        add_core_kernel, "add_core", ((two[0], F32), two, two, two), at, keep, swap(send, "core"), scalars=1
    )
    return keep, [lax.ppermute(send, "z", ring(4, step)) for step, send in zip(Z_STEPS, sends)], sends[-1], first


def sum_z(at, keep, got, after):
    one = ((128, 512), BF)
    keep, send = whole(
        add_z_kernel, "add_z", ((one[0], F32), one), at, keep, *got, scalars=1, after=after
    )
    return keep, swap(send, "xh")


def live_bias(rand, glob):
    kb = jnp.arange(NB, dtype=jnp.int32)[:, None]
    qb = jnp.arange(NB, dtype=jnp.int32)[None, :]
    live = (jnp.abs(kb - qb) <= 1) | jnp.any(kb[:, :, None] == glob[None, None, :], axis=-1)
    by_rand = jnp.any(rand.transpose(0, 2, 1)[:, :, None, :] == kb[None, None], axis=1)
    bias = jnp.where(live[None] | by_rand, 0.0, MASKED).astype(F32)
    return jnp.repeat(bias, BLK, axis=2)


TILE = 512
STEP = TILE // 128


def scores_at(k, q, bias):
    s = dot(k, q, NT).reshape(NB, BLK, TILE)
    return s * (SCALE * LOG2E) + bias[:, None, :]


def forward_kernel(qkv_ref, bias_ref, *refs):
    o_ref, stat_ref = refs[-2:]
    k = qkv_ref[:, 128:256].reshape(LEN, HS)
    v_t = qkv_ref[:, 256:384].reshape(LEN, HS).T
    for t in range(LEN // TILE):
        tok = slice(TILE * t, TILE * t + TILE)
        q = qkv_ref[STEP * t : STEP * t + STEP, :128].reshape(TILE, HS)
        s = scores_at(k, q, bias_ref[0, :, tok])
        top = jnp.max(s, axis=(0, 1), keepdims=True)
        p = jnp.exp2(s - top)
        total = jnp.sum(p, axis=(0, 1), keepdims=True)
        o_t = dot(v_t, p.astype(BF).reshape(LEN, TILE)) * (1.0 / total[0])
        o_ref[tok, :] = o_t.T.astype(BF)
        stat_ref[0, :, tok] = (top + jnp.log2(total))[0]


def forward(qkv, bias, after):
    return pl.pallas_call(
        forward_kernel,
        grid=(2,),
        in_specs=[
            pl.BlockSpec((8, QKV, HS), lambda h: (0, 0, h)),
            pl.BlockSpec((1, NB, LEN), lambda h: (h, 0, 0)),
            *[HBM] * len(after),
        ],
        out_specs=[
            pl.BlockSpec((LEN, HS), lambda h: (0, h)),
            pl.BlockSpec((1, 1, LEN), lambda h: (h, 0, 0)),
        ],
        out_shape=[
            jax.ShapeDtypeStruct((LEN, 2 * HS), BF),
            jax.ShapeDtypeStruct((2, 1, LEN), F32),
        ],
        compiler_params=params(),
        cost_estimate=pl.CostEstimate(flops=9 * 10**9, bytes_accessed=1, transcendentals=0),
        name="attention_forward",
    )(qkv, bias, *after)


def backward_kernel(at_ref, qkv_ref, bias_ref, stat_ref, o_ref, keep_ref, recv_ref, *refs):
    out_ref, dk_ref, dv_ref = refs[-3:]
    k = qkv_ref[:, 128:256].reshape(LEN, HS)
    v = qkv_ref[:, 256:384].reshape(LEN, HS)
    k_t = k.T
    for t in range(LEN // TILE):
        tok = slice(TILE * t, TILE * t + TILE)
        q = qkv_ref[STEP * t : STEP * t + STEP, :128].reshape(TILE, HS)
        half, part = divmod(TILE * t, 512)
        part = slice(part, part + TILE)
        do = jnp.where(at_ref[3] == half, keep_ref[part, :], recv_ref[part, :])
        delta = jnp.sum((do.astype(F32) * o_ref[tok, :].astype(F32)).T, axis=0, keepdims=True)
        p = jnp.exp2(scores_at(k, q, bias_ref[0, :, tok] - stat_ref[0, :, tok]))
        p = p.reshape(LEN, TILE)
        dp = dot(v, do, NT)
        ds = (p * (dp - delta)).astype(BF)
        dq = dot(k_t, ds).T * SCALE
        out_ref[STEP * t : STEP * t + STEP, :128] = dq.astype(BF).reshape(STEP, 128, HS)
        dk = dot(ds, q)
        dv = dot(p.astype(BF), do)
        if t == 0:
            dk_ref[...] = dk
            dv_ref[...] = dv
        else:
            dk_ref[...] += dk
            dv_ref[...] += dv
    out_ref[:, 128:256] = (dk_ref[...] * SCALE).astype(BF).reshape(8, 128, HS)
    out_ref[:, 256:384] = dv_ref[...].astype(BF).reshape(8, 128, HS)


def backward(at, qkv, bias, stat, attended, keep, recv, after):
    wide = pl.BlockSpec((LEN, HS), lambda h: (0, h))
    half = pl.BlockSpec((512, HS), lambda h: (0, h))
    heads = pl.BlockSpec((8, QKV, HS), lambda h: (0, 0, h))
    return pl.pallas_call(
        backward_kernel,
        grid=(2,),
        in_specs=[
            SMEM,
            heads,
            pl.BlockSpec((1, NB, LEN), lambda h: (h, 0, 0)),
            pl.BlockSpec((1, 1, LEN), lambda h: (h, 0, 0)),
            wide,
            half,
            half,
            *[HBM] * len(after),
        ],
        out_specs=heads,
        out_shape=jax.ShapeDtypeStruct((8, QKV, 2 * HS), BF),
        scratch_shapes=[pltpu.VMEM((LEN, HS), F32), pltpu.VMEM((LEN, HS), F32)],
        compiler_params=params(),
        cost_estimate=pl.CostEstimate(flops=1, bytes_accessed=1, transcendentals=0),
        name="attention_backward",
    )(at, qkv, bias, stat, attended, keep, recv, *after)


def unpack_kernel(in_ref, q_ref, k_ref, v_ref, rows_ref):
    for c in range(8):
        cols = slice(256 * c, 256 * c + 256)
        for j, ref in enumerate((q_ref, k_ref, v_ref)):
            ref[:, cols] = in_ref[c, 128 * j : 128 * j + 128]
    for side in range(2):
        for y in range(4):
            first = in_ref[4 * side + y, QKV : QKV + 16].astype(F32)
            second = in_ref[4 * (1 - side) + y, QKV + 16 :].astype(F32)
            rows_ref[:, 1024 * side + 256 * y : 1024 * side + 256 * y + 256] = first + second


def unpack_heads(grads):
    out = ((128, HD), BF)
    return whole(unpack_kernel, "unpack_heads", (out, out, out, ((16, HD), F32)), grads)


def on_device(queries, keys, values, out_weight, cotangent, rand_blocks, glob_blocks):
    at = jnp.stack([lax.axis_index(name) for name in DP + CTX]).astype(jnp.int32)
    xl = at[3]
    cot = near_cot(cotangent[0])
    weight, early = gather_weight(at, out_weight)
    qkv = hold(pack_heads(queries[0], keys[0], values[0]), (early, *cot[1:3]))
    qkv = lax.all_to_all(qkv, CTX, 0, 0, tiled=True)

    bias = live_bias(rand_blocks[0], glob_blocks[0])
    attended, stat = forward(qkv, bias, ())
    cot += far_cot(cot[1], cot[2], (stat,))
    other = swap(lax.dynamic_slice(attended, (512 * (1 - xl), 0), (512, 256)))
    part = mixed_parts(at, attended, other, weight, ())
    rows, got, started, first = weight_grad(at, cot, attended, other, (part,))
    keep, send = head_cot_parts(at, cot, weight, (first,))
    part = lax.all_to_all(part, "y", 0, 0, tiled=True)
    grads = backward(at, qkv, bias, stat, attended, keep, swap(send), (started,))
    rows, rows_recv = sum_z(at, rows, got, (grads,))
    total_tokens = lax.axis_size(DP) * lax.axis_size(CTX) * cotangent.shape[1]
    grads = attach(rows, rows_recv, grads, 1.0 / math.sqrt(total_tokens))
    grads = lax.all_to_all(grads, CTX, 0, 0, tiled=True)

    mixed = finish_mixed(part)
    grad_q, grad_k, grad_v, grad_w = unpack_heads(grads)
    return (mixed[None], grad_q[None], grad_k[None], grad_v[None], grad_w)


def solution(mesh):
    fine = Mesh(mesh.devices.reshape(4, 2, 2, 2, 4), ("z", "xh", "core", "xl", "y"))
    tokens = P(DP, CTX, None)
    return jax.shard_map(
        on_device,
        mesh=fine,
        in_specs=(tokens, tokens, tokens, P(DP + CTX, None), tokens, P(DP, CTX, None, None), P(DP, None)),
        out_specs=(tokens, tokens, tokens, tokens, P(DP + CTX, None)),
        check_vma=False,
    )
```
